512 devices in a mesh: res: 128 (over x_lo, z, y), seq: 4 (over x_hi, core).
Axes of the slice: x: 4 (x_hi: 2, x_lo: 2; x = x_hi * 2 + x_lo), y: 8, z: 8, core: 2. Of those that a mesh axis runs over, the one named last changes fastest.
Arguments:
- left_proj: bfloat16 [256, 2048], P('res', 'seq'), may hold values from -6 to 6
- right_proj: bfloat16 [256, 2048], P('res', 'seq'), may hold values from -6 to 6
- pair_cotangent: bfloat16 [256, 256, 128], P('res'), may hold values from -3 to 3
- out_weight: bfloat16 [1024, 128], replicated, may hold values from -1.5 to 1.5
- out_bias: float32 [128], replicated, may hold values from -1.8 to 1.8
Outputs:
- pair_update: bfloat16 [256, 256, 128], P('res', 'seq')
- grad_left: float32 [256, 2048], P('res', 'seq')
- grad_right: float32 [256, 2048], P('res', 'seq')
- grad_weight: float32 [1024, 128], P('res')
- grad_bias: float32 [128], replicated
The draws below stay inside these ranges and needn't reach their ends.
All inputs are finite; a program needn't handle non-finite values.
Results may differ from the reference program's by a relative error of at most 0.003.
Values may be sent and summed in bfloat16 or wider, within the bound.
No kernel may reach another device: no remote copies, remote signals or barrier semaphores. Data moves between devices by JAX's collectives and lax.ppermute only.
A program may use at most 64 MiB of HBM per device.

```python
import math
import jax
import jax.numpy as jnp
from jax import lax

C = 32
P_SIZE = 128
CC = 1024
S = 64
R = 256
WINDOW = 256


def raised(values, stream_key, source, target, blocks, factor):
    def block_of(position):
        return (jnp.arange(values.shape[position]) // (values.shape[position] // blocks)).reshape((-1,) + (1,) * (values.ndim - 1 - position))

    first = jax.random.permutation(stream_key, blocks)[block_of(target)]
    far = (block_of(target) + blocks // 2) % blocks
    return jnp.where((block_of(source) == first) | (block_of(source) == far), factor * values, values)


def steps_of(stream_key, shape, shards, low, top_value):
    factor_of = 1.0
    for position, parts in shards:
        draws = jax.random.uniform(jax.random.fold_in(jax.random.fold_in(stream_key, 6), position), (parts,), jnp.float32, low / len(shards), top_value / len(shards))
        factor_of = factor_of * jnp.repeat(jnp.exp(draws), shape[position] // parts).reshape((-1,) + (1,) * (len(shape) - 1 - position))
    return factor_of


def centred(rng, shape, scale, bound, cuts=(), kind=jnp.bfloat16):
    entries = scale * jax.random.normal(rng, shape, jnp.float32)
    if cuts:
        entries = entries * steps_of(rng, shape, cuts, -0.22, 0.18)
    return jnp.clip(entries, -bound, bound).astype(kind)


def gaussian_with(key, shape, deviation, reach, pieces, heavy, held_as=jnp.bfloat16):
    drawn = deviation * jax.random.normal(key, shape, jnp.float32)
    if pieces:
        drawn = drawn * steps_of(key, shape, pieces, -0.22, 0.18)
    return jnp.clip(raised(drawn, jax.random.fold_in(key, 3), *heavy), -reach, reach).astype(held_as)


def setup_inputs(seed: int = 0) -> dict:
    key_list = jax.random.split(jax.random.key(seed), 6)
    return {
        "left_proj": centred(key_list[0], (WINDOW, S * C), 1.0, 6.0, ((0, 128), (1, 4))),
        "right_proj": centred(key_list[1], (R, S * C), 1.0, 6.0, ((0, 128), (1, 4))),
        "pair_cotangent": gaussian_with(key_list[2], (WINDOW, R, P_SIZE), 0.125, 3.0, ((0, 128),), (0, 1, 128, 5.5)),
        "out_weight": centred(key_list[3], (CC, P_SIZE), (CC // S) ** -0.5, 1.5),
        "out_bias": centred(key_list[4], (P_SIZE,), 0.3, 1.8, (), jnp.float32),
    }


def reference(left_proj, right_proj, pair_cotangent, out_weight, out_bias):
    highest = lax.Precision.HIGHEST
    block = math.gcd(WINDOW, 16)
    left_all = left_proj.astype(jnp.float32).reshape(WINDOW // block, block, S, C)
    right_all = right_proj.astype(jnp.float32).reshape(R, S, C)
    cotan_blocks = pair_cotangent.reshape(WINDOW // block, block, R, P_SIZE)
    weight_wide = out_weight.astype(jnp.float32)
    weight_back = out_weight.T

    def row_block(totals, inputs):
        grad_right, grad_weight = totals
        left_block, cotan_block = inputs
        products = jnp.einsum("isx,jsy->ijxy", left_block, right_all, precision=highest) / S
        flat_outer = products.reshape(block * R, C * C)
        mixed_rows = jnp.dot(flat_outer, weight_wide, precision=highest).reshape(block, R, P_SIZE)
        update = (mixed_rows + out_bias).astype(jnp.bfloat16)
        flat_cotan = cotan_block.reshape(block * R, P_SIZE)
        spread_low = jnp.dot(flat_cotan, weight_back, preferred_element_type=jnp.float32).astype(jnp.bfloat16)
        spread = lax.optimization_barrier(spread_low).astype(jnp.float32).reshape(block, R, C, C)
        grad_left = jnp.einsum("jsy,ijxy->isx", right_all, spread, precision=highest) / S
        grad_right = grad_right + jnp.einsum("isx,ijxy->jsy", left_block, spread, precision=highest)
        grad_weight = grad_weight + jnp.dot(flat_outer.T, flat_cotan.astype(jnp.float32), precision=highest)
        return (grad_right, grad_weight), (update, grad_left)

    initial = (jnp.zeros((R, S, C), jnp.float32), jnp.zeros((C * C, P_SIZE), jnp.float32))
    totals, outputs = lax.scan(row_block, initial, (left_all, cotan_blocks))
    grad_right, grad_weight = totals
    pair_update = outputs[0].reshape(WINDOW, R, P_SIZE)
    grad_left = outputs[1].reshape(WINDOW, S * C)
    grad_right = (grad_right / S).reshape(R, S * C)
    grad_bias = jnp.sum(pair_cotangent.astype(jnp.float32), axis=(0, 1))
    return pair_update, grad_left, grad_right, grad_weight, grad_bias
```

```python
import jax
import jax.numpy as jnp
from jax import lax
from jax.sharding import PartitionSpec as P

C = 32
P_SIZE = 128
SEQ_DEV = 16
ROW_DEV = 2
WIDE = SEQ_DEV * C


def hi_lo(value):
    high = lax.reduce_precision(value, 8, 7)
    return high.astype(jnp.bfloat16), (value - high).astype(jnp.bfloat16)


def dot32(form, a, b):
    return jnp.einsum(form, a, b, preferred_element_type=jnp.float32)


def on_device(left_proj, right_proj, pair_cotangent, out_weight, out_bias):
    res = lax.axis_size("res")
    seq = lax.axis_size("seq")
    scale = 1.0 / (SEQ_DEV * seq)
    left_rows = left_proj.reshape(ROW_DEV, SEQ_DEV, C)
    weight = out_weight.reshape(C, C, P_SIZE)

    mixed_hi, mixed_lo = hi_lo(dot32("isx,xyk->isyk", left_rows, weight))
    grad_right = dot32("ijk,isyk->jsy", pair_cotangent, mixed_hi) + dot32(
        "ijk,isyk->jsy", pair_cotangent, mixed_lo
    )
    bias_pair = jnp.stack(hi_lo(jnp.sum(pair_cotangent, axis=(0, 1), dtype=jnp.float32)))

    message = jnp.concatenate(
        [
            jnp.broadcast_to(right_proj[None], (res, ROW_DEV, WIDE)),
            grad_right.reshape(res, ROW_DEV, WIDE).astype(jnp.bfloat16),
            jnp.broadcast_to(bias_pair[None], (res, 2, P_SIZE)),
        ],
        axis=2,
    )
    arrived = lax.all_to_all(message, "res", 0, 0, tiled=True)
    right_all = arrived[:, :, :WIDE].reshape(res * ROW_DEV, SEQ_DEV, C)
    grad_right = jnp.sum(arrived[:, :, WIDE : 2 * WIDE], axis=0, dtype=jnp.float32) * scale
    grad_bias = jnp.sum(arrived[:, :, 2 * WIDE :], axis=(0, 1), dtype=jnp.float32)

    pair = dot32("jsy,isyk->ijk", right_all, mixed_hi) + dot32("jsy,isyk->ijk", right_all, mixed_lo)
    back_hi, back_lo = hi_lo(dot32("jsy,ijk->isyk", right_all, pair_cotangent))
    grad_left = dot32("isyk,xyk->isx", back_hi, weight) + dot32("isyk,xyk->isx", back_lo, weight)
    grad_weight = dot32("isx,isyk->xyk", left_rows, back_hi) + dot32("isx,isyk->xyk", left_rows, back_lo)

    rows = C * C // res
    parts = lax.all_to_all(
        grad_weight.reshape(res, rows, P_SIZE).astype(jnp.bfloat16), "res", 0, 0, tiled=True
    )
    weight_sum = jnp.sum(parts, axis=0, dtype=jnp.float32)

    cols = pair.shape[1] // seq
    pair = jnp.moveaxis(pair.reshape(ROW_DEV, seq, cols, P_SIZE), 1, 0)
    last = jnp.concatenate(
        [
            pair.reshape(seq, ROW_DEV * cols, P_SIZE),
            jnp.broadcast_to(weight_sum[None], (seq, rows, P_SIZE)),
        ],
        axis=1,
    )
    summed = jnp.sum(lax.all_to_all(last, "seq", 0, 0, tiled=True), axis=0) * scale
    pair_update = (summed[: ROW_DEV * cols].reshape(ROW_DEV, cols, P_SIZE) + out_bias).astype(jnp.bfloat16)
    return (
        pair_update,
        (grad_left * scale).reshape(ROW_DEV, WIDE),
        grad_right,
        summed[ROW_DEV * cols :],
        grad_bias,
    )


def solution(mesh):
    return jax.shard_map(
        on_device,
        mesh=mesh,
        in_specs=(P("res", "seq"), P("res", "seq"), P("res", None, None), P(), P()),
        out_specs=(P("res", "seq", None), P("res", "seq"), P("res", "seq"), P("res", None), P()),
        check_vma=False,
    )
```

```python
import jax
import jax.numpy as jnp
from jax import lax
from jax.sharding import PartitionSpec as P

C = 32
P_SIZE = 128
SEQ_DEV = 16
ROW_DEV = 2
WIDE = SEQ_DEV * C


def hi_lo(value):
    high = lax.reduce_precision(value, 8, 7)
    return high.astype(jnp.bfloat16), (value - high).astype(jnp.bfloat16)


def dot32(form, a, b):
    return jnp.einsum(form, a, b, preferred_element_type=jnp.float32)


def on_device(left_proj, right_proj, pair_cotangent, out_weight, out_bias):
    res = lax.axis_size("res")
    seq = lax.axis_size("seq")
    scale = 1.0 / (SEQ_DEV * seq)
    left_rows = left_proj.reshape(ROW_DEV, SEQ_DEV, C)
    weight = out_weight.reshape(C, C, P_SIZE)

    right_all = lax.all_to_all(
        jnp.broadcast_to(right_proj[None], (res, ROW_DEV, WIDE)), "res", 0, 0, tiled=True
    ).reshape(res * ROW_DEV, SEQ_DEV, C)

    mixed_hi, mixed_lo = hi_lo(dot32("isx,xyk->isyk", left_rows, weight))
    grad_right = dot32("ijk,isyk->jsy", pair_cotangent, mixed_hi) + dot32(
        "ijk,isyk->jsy", pair_cotangent, mixed_lo
    )
    grad_right = grad_right.astype(jnp.bfloat16).reshape(res, ROW_DEV, WIDE)
    bias_pair = jnp.stack(hi_lo(jnp.sum(pair_cotangent, axis=(0, 1), dtype=jnp.float32)))
    bias_pair = jnp.broadcast_to(bias_pair[None], (res, 2, P_SIZE))

    back_hi, back_lo = hi_lo(dot32("jsy,ijk->isyk", right_all, pair_cotangent))
    grad_weight = dot32("isx,isyk->xyk", left_rows, back_hi) + dot32("isx,isyk->xyk", left_rows, back_lo)
    rows = C * C // res
    grad_weight = grad_weight.astype(jnp.bfloat16).reshape(res, ROW_DEV, rows * P_SIZE // ROW_DEV)

    parts = lax.all_to_all(
        jnp.concatenate([grad_right, grad_weight, bias_pair], axis=2), "res", 0, 0, tiled=True
    )

    grad_left = dot32("isyk,xyk->isx", back_hi, weight) + dot32("isyk,xyk->isx", back_lo, weight)
    pair = dot32("jsy,isyk->ijk", right_all, mixed_hi) + dot32("jsy,isyk->ijk", right_all, mixed_lo)
    cols = pair.shape[1] // seq
    pair = jnp.moveaxis(pair.reshape(ROW_DEV, seq, cols, P_SIZE), 1, 0).reshape(seq, ROW_DEV * cols, P_SIZE)
    pair_sent, pair_rest = hi_lo(pair)
    pair_rest = lax.dynamic_index_in_dim(pair_rest, lax.axis_index("seq"), 0, keepdims=False)

    totals = jnp.sum(parts, axis=0, dtype=jnp.float32)
    grad_right = totals[:, :WIDE] * scale
    weight_hi, weight_lo = hi_lo(totals[:, WIDE : WIDE + rows * P_SIZE // ROW_DEV].reshape(rows, P_SIZE))
    grad_bias = totals[0, -P_SIZE:] + totals[1, -P_SIZE:]

    last = jnp.concatenate(
        [
            pair_sent,
            jnp.broadcast_to(weight_hi[None], (seq, rows, P_SIZE)),
            jnp.broadcast_to(weight_lo[None], (seq, rows, P_SIZE)),
        ],
        axis=1,
    )
    summed = jnp.sum(lax.all_to_all(last, "seq", 0, 0, tiled=True), axis=0, dtype=jnp.float32) * scale
    split = ROW_DEV * cols
    pair_update = (summed[:split] + pair_rest * scale).reshape(ROW_DEV, cols, P_SIZE) + out_bias
    return (
        pair_update.astype(jnp.bfloat16),
        (grad_left * scale).reshape(ROW_DEV, WIDE),
        grad_right,
        summed[split : split + rows] + summed[split + rows :],
        grad_bias,
    )


def solution(mesh):
    return jax.shard_map(
        on_device,
        mesh=mesh,
        in_specs=(P("res", "seq"), P("res", "seq"), P("res", None, None), P(), P()),
        out_specs=(P("res", "seq", None), P("res", "seq"), P("res", "seq"), P("res", None), P()),
        check_vma=False,
    )
```

```python
import jax
import jax.numpy as jnp
from jax import lax
from jax.sharding import PartitionSpec as P

C = 32
P_SIZE = 128
SEQ_DEV = 16
ROW_DEV = 2
WIDE = SEQ_DEV * C


def hi_lo(value):
    high = lax.reduce_precision(value, 8, 7)
    return high.astype(jnp.bfloat16), (value - high).astype(jnp.bfloat16)


def dot32(form, a, b):
    return jnp.einsum(form, a, b, preferred_element_type=jnp.float32)


def on_device(left_proj, right_proj, pair_cotangent, out_weight, out_bias):
    res = lax.axis_size("res")
    seq = lax.axis_size("seq")
    scale = 1.0 / (SEQ_DEV * seq)
    left_rows = left_proj.reshape(ROW_DEV, SEQ_DEV, C)
    weight = out_weight.reshape(C, C, P_SIZE)

    right_all = lax.all_to_all(
        jnp.broadcast_to(right_proj[None], (res, ROW_DEV, WIDE)), "res", 0, 0, tiled=True
    ).reshape(res * ROW_DEV, SEQ_DEV, C)

    mixed_hi, mixed_lo = hi_lo(dot32("isx,xyk->isyk", left_rows, weight))
    grad_right = dot32("ijk,isyk->jsy", pair_cotangent, mixed_hi) + dot32(
        "ijk,isyk->jsy", pair_cotangent, mixed_lo
    )
    grad_right = grad_right.astype(jnp.bfloat16).reshape(res, ROW_DEV, WIDE)
    bias_pair = jnp.stack(hi_lo(jnp.sum(pair_cotangent, axis=(0, 1), dtype=jnp.float32)))
    bias_pair = jnp.broadcast_to(bias_pair[None], (res, 2, P_SIZE))

    back_hi, back_lo = hi_lo(dot32("jsy,ijk->isyk", right_all, pair_cotangent))
    grad_weight = dot32("isx,isyk->xyk", left_rows, back_hi) + dot32("isx,isyk->xyk", left_rows, back_lo)
    rows = C * C // res
    grad_weight = grad_weight.astype(jnp.bfloat16).reshape(res, ROW_DEV, rows * P_SIZE // ROW_DEV)

    message = jnp.concatenate([grad_right, grad_weight, bias_pair], axis=2)
    message, right_all = lax.optimization_barrier((message, right_all))
    parts = lax.all_to_all(message, "res", 0, 0, tiled=True)

    grad_left = dot32("isyk,xyk->isx", back_hi, weight) + dot32("isyk,xyk->isx", back_lo, weight)
    pair = dot32("jsy,isyk->ijk", right_all, mixed_hi) + dot32("jsy,isyk->ijk", right_all, mixed_lo)
    cols = pair.shape[1] // seq
    here = lax.axis_index("seq")

    def columns_of(owner):
        return lax.dynamic_slice_in_dim(pair, owner * cols, cols, 1)

    pair_sum = columns_of(here)
    for step in range(1, seq):
        sent = columns_of(lax.rem(here + step, seq))
        pair_sum = pair_sum + lax.ppermute(sent, "seq", [(q, (q + step) % seq) for q in range(seq)])
    pair_update = (pair_sum * scale + out_bias).astype(jnp.bfloat16)

    totals = jnp.sum(parts, axis=0, dtype=jnp.float32)
    weight_sum = totals[:, WIDE : WIDE + rows * P_SIZE // ROW_DEV].reshape(rows, P_SIZE)

    last = lax.all_to_all(jnp.broadcast_to(weight_sum[None], (seq, rows, P_SIZE)), "seq", 0, 0, tiled=True)
    return (
        pair_update,
        (grad_left * scale).reshape(ROW_DEV, WIDE),
        totals[:, :WIDE] * scale,
        jnp.sum(last, axis=0) * scale,
        totals[0, -P_SIZE:] + totals[1, -P_SIZE:],
    )


def solution(mesh):
    return jax.shard_map(
        on_device,
        mesh=mesh,
        in_specs=(P("res", "seq"), P("res", "seq"), P("res", None, None), P(), P()),
        out_specs=(P("res", "seq", None), P("res", "seq"), P("res", "seq"), P("res", None), P()),
        check_vma=False,
    )
```

```python
import jax
import jax.numpy as jnp
from jax import lax
from jax.experimental import pallas as pl
from jax.experimental.pallas import tpu as pltpu
from jax.sharding import PartitionSpec as P

C = 32
P_SIZE = 128
SEQ_DEV = 16
ROW_DEV = 2
WIDE = SEQ_DEV * C


def hi_lo(value):
    high = lax.reduce_precision(value, 8, 7)
    return high.astype(jnp.bfloat16), (value - high).astype(jnp.bfloat16)


def dot32(form, a, b):
    return jnp.einsum(form, a, b, preferred_element_type=jnp.float32)


def products_kernel(right, cotan, mixed_hi, mixed_lo, left_cols, pair, weight_out, back_hi, back_lo, back, weight_sum):
    rows = right[...]
    both = jnp.concatenate([cotan[0], cotan[1]], axis=1)
    terms = lax.dot_general(rows, both, (((0,), (0,)), ((), ())), preferred_element_type=jnp.float32)
    back[0] = terms[:, :P_SIZE]
    back[1] = terms[:, P_SIZE:]
    lhs = left_cols[...]
    for y in range(C):
        parts = []
        for i in range(ROW_DEV):
            term = back[i, pl.ds(y, SEQ_DEV, stride=C), :]
            high = term.astype(jnp.bfloat16)
            parts += [high, (term - high.astype(jnp.float32)).astype(jnp.bfloat16)]
        weight_sum[pl.ds(y, C, stride=C), :] = jnp.dot(
            lhs, jnp.concatenate(parts, axis=0), preferred_element_type=jnp.float32
        )
    weight_out[...] = weight_sum[...].astype(jnp.bfloat16)
    for i in range(ROW_DEV):
        pair[i] = jnp.dot(rows, mixed_hi[i], preferred_element_type=jnp.float32) + jnp.dot(
            rows, mixed_lo[i], preferred_element_type=jnp.float32
        )
        term = back[i]
        high = term.astype(jnp.bfloat16)
        back_hi[i] = high
        back_lo[i] = (term - high.astype(jnp.float32)).astype(jnp.bfloat16)


def products(right, cotan, mixed_hi, mixed_lo, left_cols):
    whole = pl.BlockSpec(memory_space=pltpu.VMEM)
    back = (ROW_DEV, WIDE, P_SIZE)
    return pl.pallas_call(
        products_kernel,
        out_shape=(
            jax.ShapeDtypeStruct((ROW_DEV, right.shape[0], P_SIZE), jnp.float32),
            jax.ShapeDtypeStruct((C * C, P_SIZE), jnp.bfloat16),
            jax.ShapeDtypeStruct(back, jnp.bfloat16),
            jax.ShapeDtypeStruct(back, jnp.bfloat16),
        ),
        in_specs=[whole] * 5,
        out_specs=(whole,) * 4,
        scratch_shapes=[pltpu.VMEM(back, jnp.float32), pltpu.VMEM((C * C, P_SIZE), jnp.float32)],
        compiler_params=pltpu.CompilerParams(vmem_limit_bytes=16 * 1024 * 1024),
        cost_estimate=pl.CostEstimate(flops=300_000_000, bytes_accessed=3_000_000, transcendentals=0),
    )(right, cotan, mixed_hi, mixed_lo, left_cols)


def on_device(left_proj, right_proj, pair_cotangent, out_weight, out_bias):
    res = lax.axis_size("res")
    seq = lax.axis_size("seq")
    scale = 1.0 / (SEQ_DEV * seq)
    left_rows = left_proj.reshape(ROW_DEV, SEQ_DEV, C)
    weight = out_weight.reshape(C, C, P_SIZE)

    right_all = lax.all_to_all(
        jnp.broadcast_to(right_proj[None], (res, ROW_DEV, WIDE)), "res", 0, 0, tiled=True
    ).reshape(res * ROW_DEV, WIDE)

    mixed_hi, mixed_lo = hi_lo(dot32("isx,xyk->isyk", left_rows, weight))
    grad_right = dot32("ijk,isyk->jsy", pair_cotangent, mixed_hi) + dot32(
        "ijk,isyk->jsy", pair_cotangent, mixed_lo
    )
    grad_right = grad_right.astype(jnp.bfloat16).reshape(res, ROW_DEV, WIDE)
    bias_pair = jnp.stack(hi_lo(jnp.sum(pair_cotangent, axis=(0, 1), dtype=jnp.float32)))
    bias_pair = jnp.broadcast_to(bias_pair[None], (res, 2, P_SIZE))
    rows = C * C // res
    blank = jnp.zeros((res, ROW_DEV, rows * P_SIZE // ROW_DEV), jnp.bfloat16)
    body = lax.optimization_barrier(jnp.concatenate([blank, grad_right, bias_pair], axis=2))
    left_cols = jnp.broadcast_to(left_rows.transpose(2, 0, 1)[:, :, None], (C, ROW_DEV, 2, SEQ_DEV))
    left_cols = left_cols.reshape(C, ROW_DEV * 2 * SEQ_DEV)
    mixed = (ROW_DEV, WIDE, P_SIZE)

    pair, grad_weight, back_hi, back_lo = products(
        right_all, pair_cotangent, mixed_hi.reshape(mixed), mixed_lo.reshape(mixed), left_cols
    )

    grad_weight = grad_weight.reshape(blank.shape)
    parts = lax.all_to_all(lax.dynamic_update_slice(body, grad_weight, (0, 0, 0)), "res", 0, 0, tiled=True)

    back_hi, back_lo = (term.reshape(ROW_DEV, SEQ_DEV, C, P_SIZE) for term in (back_hi, back_lo))
    grad_left = dot32("isyk,xyk->isx", back_hi, weight) + dot32("isyk,xyk->isx", back_lo, weight)
    cols = pair.shape[1] // seq
    here = lax.axis_index("seq")

    def columns_of(owner):
        return lax.dynamic_slice_in_dim(pair, owner * cols, cols, 1)

    pair_sum = columns_of(here)
    for step in range(1, seq):
        sent = columns_of(lax.rem(here + step, seq))
        pair_sum = pair_sum + lax.ppermute(sent, "seq", [(q, (q + step) % seq) for q in range(seq)])
    pair_update = (pair_sum * scale + out_bias).astype(jnp.bfloat16)

    totals = jnp.sum(parts, axis=0, dtype=jnp.float32)
    weight_sum = totals[:, : rows * P_SIZE // ROW_DEV].reshape(rows, P_SIZE)

    last = lax.all_to_all(jnp.broadcast_to(weight_sum[None], (seq, rows, P_SIZE)), "seq", 0, 0, tiled=True)
    return (
        pair_update,
        (grad_left * scale).reshape(ROW_DEV, WIDE),
        totals[:, rows * P_SIZE // ROW_DEV : -P_SIZE] * scale,
        jnp.sum(last, axis=0) * scale,
        totals[0, -P_SIZE:] + totals[1, -P_SIZE:],
    )


def solution(mesh):
    return jax.shard_map(
        on_device,
        mesh=mesh,
        in_specs=(P("res", "seq"), P("res", "seq"), P("res", None, None), P(), P()),
        out_specs=(P("res", "seq", None), P("res", "seq"), P("res", "seq"), P("res", None), P()),
        check_vma=False,
    )
```

```python
import jax
import jax.numpy as jnp
from jax import lax
from jax.experimental import pallas as pl
from jax.experimental.pallas import tpu as pltpu
from jax.sharding import Mesh
from jax.sharding import PartitionSpec as P

C = 32
P_SIZE = 128
SEQ_DEV = 16
ROW_DEV = 2
WIDE = SEQ_DEV * C
HALVES = 2
WHOLE = pl.BlockSpec(memory_space=pltpu.VMEM)


def split_in_two(value):
    high = value.astype(jnp.bfloat16)
    return high, (value - high.astype(jnp.float32)).astype(jnp.bfloat16)


def dot32(form, a, b):
    return jnp.einsum(form, a, b, preferred_element_type=jnp.float32)


def opening_kernel(right, cotan, out):
    total = jnp.sum(cotan[...].astype(jnp.float32), axis=(0, 1))[None]
    high = total.astype(jnp.bfloat16).astype(jnp.float32)
    upper = lax.broadcasted_iota(jnp.int32, (ROW_DEV, P_SIZE), 0) == 0
    bias = jnp.where(upper, high, total - high).astype(jnp.bfloat16)
    out[:, :, :WIDE] = jnp.broadcast_to(right[...][None], (out.shape[0], ROW_DEV, WIDE))
    out[:, :, WIDE:] = jnp.broadcast_to(bias[None], (out.shape[0], ROW_DEV, P_SIZE))


def products_kernel(right, cotan, mixed_hi, mixed_lo, left_cols, grad_right, pair, message, back_hi, back_lo, back, weight):
    rows = right[...]
    both = jnp.concatenate([cotan[0], cotan[1]], axis=1)
    terms = lax.dot_general(rows, both, (((0,), (0,)), ((), ())), preferred_element_type=jnp.float32)
    back[0] = terms[:, :P_SIZE]
    back[1] = terms[:, P_SIZE:]
    lhs = left_cols[...]
    for y in range(C):
        parts = []
        for i in range(ROW_DEV):
            parts += split_in_two(back[i, pl.ds(y, SEQ_DEV, stride=C), :])
        weight[pl.ds(y, C, stride=C), :] = jnp.dot(
            lhs, jnp.concatenate(parts, axis=0), preferred_element_type=jnp.float32
        )
    planes = message.shape[0]
    own = message.shape[1] // 2
    halves = weight[...].reshape(HALVES, planes, own // HALVES, P_SIZE)
    message[:, :own, :] = jnp.concatenate([halves[0], halves[1]], axis=1).astype(jnp.bfloat16)
    message[:, own:, :] = grad_right[...]
    for i in range(ROW_DEV):
        pair[i] = jnp.dot(rows, mixed_hi[i], preferred_element_type=jnp.float32) + jnp.dot(
            rows, mixed_lo[i], preferred_element_type=jnp.float32
        )
        back_hi[i], back_lo[i] = split_in_two(back[i])


def middle_kernel(place, parts, out):
    total = jnp.sum(parts[...].astype(jnp.float32), axis=0)
    rows = total.shape[0] // 4
    seq = out.shape[0] // HALVES
    for half in range(HALVES):
        mine = total[half * rows : (half + 1) * rows]
        right = total[(half + 2) * rows : (half + 3) * rows]
        for q in range(seq):
            out[half * seq + q, :rows] = mine
            out[half * seq + q, rows:] = jnp.where(place[0] == q, right, 0.0)


def closing_kernel(scale, parts, weight, right):
    total = jnp.sum(parts[...], axis=0) * scale
    rows = weight.shape[0]
    weight[...] = total[:rows]
    for t in range(ROW_DEV):
        for m in range(rows // ROW_DEV):
            at = rows + t * (rows // ROW_DEV) + m
            right[t : t + 1, m * P_SIZE : (m + 1) * P_SIZE] = total[at : at + 1]


def on_device(left_proj, right_proj, pair_cotangent, out_weight, out_bias):
    planes = lax.axis_size("plane")
    seq = lax.axis_size("seq")
    res = HALVES * planes
    scale = 1.0 / (SEQ_DEV * seq)
    rows = C * C // res
    columns = res * ROW_DEV
    left_rows = left_proj.reshape(ROW_DEV, SEQ_DEV, C)
    weight = out_weight.reshape(C, C, P_SIZE)

    opening = pl.pallas_call(
        opening_kernel,
        out_shape=jax.ShapeDtypeStruct((res, ROW_DEV, WIDE + P_SIZE), jnp.bfloat16),
        in_specs=[WHOLE] * 2,
        out_specs=WHOLE,
        compiler_params=pltpu.CompilerParams(vmem_limit_bytes=8 * 1024 * 1024),
    )(right_proj, pair_cotangent)
    arrived = lax.all_to_all(opening, ("half", "plane"), 0, 0, tiled=True)
    right_all = arrived[:, :, :WIDE].reshape(columns, WIDE)
    grad_bias = jnp.sum(arrived[:, :, WIDE:], axis=(0, 1), dtype=jnp.float32)

    mixed = dot32("isx,xyk->isyk", left_rows, weight)
    high = lax.reduce_precision(mixed, 8, 7)
    mixed_hi, mixed_lo = high.astype(jnp.bfloat16), (mixed - high).astype(jnp.bfloat16)
    grad_right = dot32("ijk,isyk->jsy", pair_cotangent, mixed_hi) + dot32("ijk,isyk->jsy", pair_cotangent, mixed_lo)
    grad_right = grad_right.astype(jnp.bfloat16).reshape(HALVES, planes, rows, P_SIZE)
    grad_right = jnp.moveaxis(grad_right, 0, 1).reshape(planes, HALVES * rows, P_SIZE)
    left_cols = jnp.broadcast_to(left_rows.transpose(2, 0, 1)[:, :, None], (C, ROW_DEV, 2, SEQ_DEV))
    left_cols = left_cols.reshape(C, ROW_DEV * 2 * SEQ_DEV)

    back = (ROW_DEV, WIDE, P_SIZE)
    pair, message, back_hi, back_lo = pl.pallas_call(
        products_kernel,
        out_shape=(
            jax.ShapeDtypeStruct((ROW_DEV, columns, P_SIZE), jnp.float32),
            jax.ShapeDtypeStruct((planes, 2 * HALVES * rows, P_SIZE), jnp.bfloat16),
            jax.ShapeDtypeStruct(back, jnp.bfloat16),
            jax.ShapeDtypeStruct(back, jnp.bfloat16),
        ),
        in_specs=[WHOLE] * 6,
        out_specs=(WHOLE,) * 4,
        scratch_shapes=[pltpu.VMEM(back, jnp.float32), pltpu.VMEM((C * C, P_SIZE), jnp.float32)],
        compiler_params=pltpu.CompilerParams(vmem_limit_bytes=16 * 1024 * 1024),
        cost_estimate=pl.CostEstimate(flops=300_000_000, bytes_accessed=3_000_000, transcendentals=0),
    )(right_all, pair_cotangent, mixed_hi.reshape(back), mixed_lo.reshape(back), left_cols, grad_right)

    parts = lax.all_to_all(message, "plane", 0, 0, tiled=True)

    back_hi, back_lo = (term.reshape(ROW_DEV, SEQ_DEV, C, P_SIZE) for term in (back_hi, back_lo))
    grad_left = dot32("isyk,xyk->isx", back_hi, weight) + dot32("isyk,xyk->isx", back_lo, weight)
    cols = columns // seq
    here = lax.axis_index("seq")

    def columns_of(owner):
        return lax.dynamic_slice_in_dim(pair, owner * cols, cols, 1)

    pair_sum = columns_of(here)
    for step in range(1, seq):
        sent = columns_of(lax.bitwise_xor(here, jnp.int32(step)))
        pair_sum = pair_sum + lax.ppermute(sent, "seq", [(q, q ^ step) for q in range(seq)])
    pair_update = (pair_sum * scale + out_bias).astype(jnp.bfloat16)

    last = pl.pallas_call(
        middle_kernel,
        out_shape=jax.ShapeDtypeStruct((HALVES * seq, 2 * rows, P_SIZE), jnp.float32),
        in_specs=[pl.BlockSpec(memory_space=pltpu.SMEM), WHOLE],
        out_specs=WHOLE,
        compiler_params=pltpu.CompilerParams(vmem_limit_bytes=8 * 1024 * 1024),
    )(here.reshape(1), parts)
    last = lax.all_to_all(last, ("half", "seq"), 0, 0, tiled=True)
    grad_weight, grad_right = pl.pallas_call(
        lambda *refs: closing_kernel(scale, *refs),
        out_shape=(
            jax.ShapeDtypeStruct((rows, P_SIZE), jnp.float32),
            jax.ShapeDtypeStruct((ROW_DEV, WIDE), jnp.float32),
        ),
        in_specs=[WHOLE],
        out_specs=(WHOLE,) * 2,
        compiler_params=pltpu.CompilerParams(vmem_limit_bytes=8 * 1024 * 1024),
    )(last)
    return pair_update, (grad_left * scale).reshape(ROW_DEV, WIDE), grad_right, grad_weight, grad_bias


def solution(mesh):
    res, seq = mesh.devices.shape
    fine = Mesh(mesh.devices.reshape(HALVES, res // HALVES, seq), ("half", "plane", "seq"))
    across = ("half", "plane")
    return jax.shard_map(
        on_device,
        mesh=fine,
        in_specs=(P(across, "seq"), P(across, "seq"), P(across, None, None), P(), P()),
        out_specs=(P(across, "seq", None), P(across, "seq"), P(across, "seq"), P(across, None), P()),
        check_vma=False,
    )
```

```python
import jax
import jax.numpy as jnp
from jax import lax
from jax.experimental import pallas as pl
from jax.experimental.pallas import tpu as pltpu
from jax.sharding import Mesh
from jax.sharding import PartitionSpec as P

C = 32
P_SIZE = 128
SEQ_DEV = 16
ROW_DEV = 2
WIDE = SEQ_DEV * C
HALVES = 2
WHOLE = pl.BlockSpec(memory_space=pltpu.VMEM)


def split_in_two(value):
    high = value.astype(jnp.bfloat16)
    return high, (value - high.astype(jnp.float32)).astype(jnp.bfloat16)


def dot32(form, a, b):
    return jnp.einsum(form, a, b, preferred_element_type=jnp.float32)


def opening_kernel(right, cotan, out):
    total = jnp.sum(cotan[...].astype(jnp.float32), axis=(0, 1))[None]
    high = total.astype(jnp.bfloat16).astype(jnp.float32)
    upper = lax.broadcasted_iota(jnp.int32, (ROW_DEV, P_SIZE), 0) == 0
    bias = jnp.where(upper, high, total - high).astype(jnp.bfloat16)
    out[:, :, :WIDE] = jnp.broadcast_to(right[...][None], (out.shape[0], ROW_DEV, WIDE))
    out[:, :, WIDE:] = jnp.broadcast_to(bias[None], (out.shape[0], ROW_DEV, P_SIZE))


def products_kernel(right, cotan, left_cols, grad_right, message, back, weight):
    rows = right[...]
    both = jnp.concatenate([cotan[0], cotan[1]], axis=1)
    terms = lax.dot_general(rows, both, (((0,), (0,)), ((), ())), preferred_element_type=jnp.float32)
    back[0] = terms[:, :P_SIZE]
    back[1] = terms[:, P_SIZE:]
    lhs = left_cols[...]
    for y in range(C):
        parts = []
        for i in range(ROW_DEV):
            parts += split_in_two(back[i, pl.ds(y, SEQ_DEV, stride=C), :])
        weight[pl.ds(y, C, stride=C), :] = jnp.dot(
            lhs, jnp.concatenate(parts, axis=0), preferred_element_type=jnp.float32
        )
    planes = message.shape[0]
    own = message.shape[1] // 2
    halves = weight[...].reshape(HALVES, planes, own // HALVES, P_SIZE)
    message[:, :own, :] = jnp.concatenate([halves[0], halves[1]], axis=1).astype(jnp.bfloat16)
    message[:, own:, :] = grad_right[...]


def pair_kernel(right, mixed_hi, mixed_lo, back, pair, back_hi, back_lo):
    rows = right[...]
    for i in range(ROW_DEV):
        pair[i] = jnp.dot(rows, mixed_hi[i], preferred_element_type=jnp.float32) + jnp.dot(
            rows, mixed_lo[i], preferred_element_type=jnp.float32
        )
        back_hi[i], back_lo[i] = split_in_two(back[i])


def middle_kernel(place, parts, out):
    total = jnp.sum(parts[...].astype(jnp.float32), axis=0)
    rows = total.shape[0] // 4
    seq = out.shape[0] // HALVES
    for half in range(HALVES):
        mine = total[half * rows : (half + 1) * rows]
        right = total[(half + 2) * rows : (half + 3) * rows]
        for q in range(seq):
            out[half * seq + q, :rows] = mine
            out[half * seq + q, rows:] = jnp.where(place[0] == q, right, 0.0)


def closing_kernel(scale, parts, weight, right):
    total = jnp.sum(parts[...], axis=0) * scale
    rows = weight.shape[0]
    weight[...] = total[:rows]
    for t in range(ROW_DEV):
        for m in range(rows // ROW_DEV):
            at = rows + t * (rows // ROW_DEV) + m
            right[t : t + 1, m * P_SIZE : (m + 1) * P_SIZE] = total[at : at + 1]


def on_device(left_proj, right_proj, pair_cotangent, out_weight, out_bias):
    planes = lax.axis_size("plane")
    seq = lax.axis_size("seq")
    res = HALVES * planes
    scale = 1.0 / (SEQ_DEV * seq)
    rows = C * C // res
    columns = res * ROW_DEV
    left_rows = left_proj.reshape(ROW_DEV, SEQ_DEV, C)
    weight = out_weight.reshape(C, C, P_SIZE)

    opening = pl.pallas_call(
        opening_kernel,
        out_shape=jax.ShapeDtypeStruct((res, ROW_DEV, WIDE + P_SIZE), jnp.bfloat16),
        in_specs=[WHOLE] * 2,
        out_specs=WHOLE,
    )(right_proj, pair_cotangent)
    arrived = lax.all_to_all(opening, ("half", "plane"), 0, 0, tiled=True)
    right_all = arrived[:, :, :WIDE].reshape(columns, WIDE)
    grad_bias = jnp.sum(arrived[:, :, WIDE:], axis=(0, 1), dtype=jnp.float32)

    mixed = dot32("isx,xyk->isyk", left_rows, weight)
    high = lax.reduce_precision(mixed, 8, 7)
    mixed_hi, mixed_lo = high.astype(jnp.bfloat16), (mixed - high).astype(jnp.bfloat16)
    grad_right = dot32("ijk,isyk->jsy", pair_cotangent, mixed_hi) + dot32("ijk,isyk->jsy", pair_cotangent, mixed_lo)
    grad_right = grad_right.astype(jnp.bfloat16).reshape(HALVES, planes, rows, P_SIZE)
    grad_right = jnp.moveaxis(grad_right, 0, 1).reshape(planes, HALVES * rows, P_SIZE)
    left_cols = jnp.broadcast_to(left_rows.transpose(2, 0, 1)[:, :, None], (C, ROW_DEV, 2, SEQ_DEV))
    left_cols = left_cols.reshape(C, ROW_DEV * 2 * SEQ_DEV)

    back = (ROW_DEV, WIDE, P_SIZE)
    message, terms = pl.pallas_call(
        products_kernel,
        out_shape=(
            jax.ShapeDtypeStruct((planes, 2 * HALVES * rows, P_SIZE), jnp.bfloat16),
            jax.ShapeDtypeStruct(back, jnp.float32),
        ),
        in_specs=[WHOLE] * 4,
        out_specs=(WHOLE,) * 2,
        scratch_shapes=[pltpu.VMEM((C * C, P_SIZE), jnp.float32)],
        compiler_params=pltpu.CompilerParams(vmem_limit_bytes=16 * 1024 * 1024),
        cost_estimate=pl.CostEstimate(flops=200_000_000, bytes_accessed=2_000_000, transcendentals=0),
    )(right_all, pair_cotangent, left_cols, grad_right)

    parts = lax.all_to_all(message, "plane", 0, 0, tiled=True)

    pair, back_hi, back_lo = pl.pallas_call(
        pair_kernel,
        out_shape=(
            jax.ShapeDtypeStruct((ROW_DEV, columns, P_SIZE), jnp.float32),
            jax.ShapeDtypeStruct(back, jnp.bfloat16),
            jax.ShapeDtypeStruct(back, jnp.bfloat16),
        ),
        in_specs=[WHOLE] * 4,
        out_specs=(WHOLE,) * 3,
        compiler_params=pltpu.CompilerParams(vmem_limit_bytes=16 * 1024 * 1024),
        cost_estimate=pl.CostEstimate(flops=150_000_000, bytes_accessed=2_000_000, transcendentals=0),
    )(right_all, mixed_hi.reshape(back), mixed_lo.reshape(back), terms)
    back_hi, back_lo = (term.reshape(ROW_DEV, SEQ_DEV, C, P_SIZE) for term in (back_hi, back_lo))
    grad_left = dot32("isyk,xyk->isx", back_hi, weight) + dot32("isyk,xyk->isx", back_lo, weight)
    cols = columns // seq
    here = lax.axis_index("seq")

    def columns_of(owner):
        return lax.dynamic_slice_in_dim(pair, owner * cols, cols, 1)

    pair_sum = columns_of(here)
    for step in range(1, seq):
        sent = columns_of(lax.bitwise_xor(here, jnp.int32(step)))
        pair_sum = pair_sum + lax.ppermute(sent, "seq", [(q, q ^ step) for q in range(seq)])
    pair_update = (pair_sum * scale + out_bias).astype(jnp.bfloat16)

    last = pl.pallas_call(
        middle_kernel,
        out_shape=jax.ShapeDtypeStruct((HALVES * seq, 2 * rows, P_SIZE), jnp.float32),
        in_specs=[pl.BlockSpec(memory_space=pltpu.SMEM), WHOLE],
        out_specs=WHOLE,
        compiler_params=pltpu.CompilerParams(vmem_limit_bytes=8 * 1024 * 1024),
    )(here.reshape(1), parts)
    last = lax.all_to_all(last, ("half", "seq"), 0, 0, tiled=True)
    grad_weight, grad_right = pl.pallas_call(
        lambda *refs: closing_kernel(scale, *refs),
        out_shape=(
            jax.ShapeDtypeStruct((rows, P_SIZE), jnp.float32),
            jax.ShapeDtypeStruct((ROW_DEV, WIDE), jnp.float32),
        ),
        in_specs=[WHOLE],
        out_specs=(WHOLE,) * 2,
        compiler_params=pltpu.CompilerParams(vmem_limit_bytes=8 * 1024 * 1024),
    )(last)
    return pair_update, (grad_left * scale).reshape(ROW_DEV, WIDE), grad_right, grad_weight, grad_bias


def solution(mesh):
    res, seq = mesh.devices.shape
    fine = Mesh(mesh.devices.reshape(HALVES, res // HALVES, seq), ("half", "plane", "seq"))
    across = ("half", "plane")
    return jax.shard_map(
        on_device,
        mesh=fine,
        in_specs=(P(across, "seq"), P(across, "seq"), P(across, None, None), P(), P()),
        out_specs=(P(across, "seq", None), P(across, "seq"), P(across, "seq"), P(across, None), P()),
        check_vma=False,
    )
```

```python
import jax
import jax.numpy as jnp
from jax import lax
from jax.experimental import pallas as pl
from jax.experimental.pallas import tpu as pltpu
from jax.sharding import Mesh
from jax.sharding import PartitionSpec as P

C = 32
P_SIZE = 128
SEQ_DEV = 16
ROW_DEV = 2
WIDE = SEQ_DEV * C
HALVES = 2
WHOLE = pl.BlockSpec(memory_space=pltpu.VMEM)


def split_in_two(value):
    high = value.astype(jnp.bfloat16)
    return high, (value - high.astype(jnp.float32)).astype(jnp.bfloat16)


def dot32(form, a, b):
    return jnp.einsum(form, a, b, preferred_element_type=jnp.float32)


def opening_kernel(right, cotan, out):
    total = jnp.sum(cotan[...].astype(jnp.float32), axis=(0, 1))[None]
    high = total.astype(jnp.bfloat16).astype(jnp.float32)
    upper = lax.broadcasted_iota(jnp.int32, (ROW_DEV, P_SIZE), 0) == 0
    bias = jnp.where(upper, high, total - high).astype(jnp.bfloat16)
    out[:, :, :WIDE] = jnp.broadcast_to(right[...][None], (out.shape[0], ROW_DEV, WIDE))
    out[:, :, WIDE:] = jnp.broadcast_to(bias[None], (out.shape[0], ROW_DEV, P_SIZE))


def right_kernel(place, cotan, mixed_hi, mixed_lo, kept, sent):
    total = jnp.zeros((cotan.shape[1], WIDE), jnp.float32)
    for i in range(ROW_DEV):
        for mixed in (mixed_hi, mixed_lo):
            total += lax.dot_general(cotan[i], mixed[i], (((1,), (1,)), ((), ())), preferred_element_type=jnp.float32)
    low, high = total[:, : WIDE // 2], total[:, WIDE // 2 :]
    kept[...] = jnp.where(place[0] == 0, low, high)
    sent[...] = jnp.where(place[0] == 0, high, low)


def packing_kernel(kept, got, out, total):
    blocks = kept.shape[1] // P_SIZE
    lines = ROW_DEV * blocks * HALVES
    planes = out.shape[0] // lines
    for m in range(blocks):
        cut = slice(m * P_SIZE, (m + 1) * P_SIZE)
        total[m] = kept[:, cut] + got[:, cut]
        for half in range(HALVES):
            for t in range(ROW_DEV):
                out[pl.ds((half * ROW_DEV + t) * blocks + m, planes, stride=lines), :] = total[
                    m, pl.ds(half * planes * ROW_DEV + t, planes, stride=ROW_DEV), :
                ]


def products_kernel(right, cotan, left_cols, grad_right, message, back, weight):
    rows = right[...]
    both = jnp.concatenate([cotan[0], cotan[1]], axis=1)
    terms = lax.dot_general(rows, both, (((0,), (0,)), ((), ())), preferred_element_type=jnp.float32)
    back[0] = terms[:, :P_SIZE]
    back[1] = terms[:, P_SIZE:]
    lhs = left_cols[...]
    for y in range(C):
        parts = []
        for i in range(ROW_DEV):
            parts += split_in_two(back[i, pl.ds(y, SEQ_DEV, stride=C), :])
        weight[pl.ds(y, C, stride=C), :] = jnp.dot(
            lhs, jnp.concatenate(parts, axis=0), preferred_element_type=jnp.float32
        )
    planes = message.shape[0]
    halves = weight[...].reshape(HALVES, planes, C * C // (HALVES * planes), P_SIZE)
    own = grad_right[...].reshape(planes, grad_right.shape[0] // planes, P_SIZE)
    message[...] = jnp.concatenate([halves[0], halves[1], own], axis=1).astype(jnp.bfloat16)


def pair_kernel(right, mixed_hi, mixed_lo, back, pair, back_hi, back_lo):
    rows = right[...]
    for i in range(ROW_DEV):
        pair[i] = jnp.dot(rows, mixed_hi[i], preferred_element_type=jnp.float32) + jnp.dot(
            rows, mixed_lo[i], preferred_element_type=jnp.float32
        )
        back_hi[i], back_lo[i] = split_in_two(back[i])


def middle_kernel(place, parts, out):
    total = jnp.sum(parts[...].astype(jnp.float32), axis=0)
    rows = total.shape[0] // 3
    seq = out.shape[0] // HALVES
    right = total[2 * rows :]
    swapped = jnp.concatenate([right[rows // 2 :], right[: rows // 2]], axis=0)
    for half in range(HALVES):
        mine = total[half * rows : (half + 1) * rows]
        for q in range(seq):
            out[half * seq + q, :rows] = mine
            out[half * seq + q, rows:] = jnp.where(place[0] == q, swapped if half else right, 0.0)


def closing_kernel(scale, parts, weight, right):
    rows = weight.shape[0]
    seq = parts.shape[0] // HALVES
    sums = [jnp.sum(parts[half * seq : (half + 1) * seq], axis=0) * scale for half in range(HALVES)]
    weight[...] = sums[0][:rows] + sums[1][:rows]
    blocks = WIDE // HALVES // P_SIZE
    for half in range(HALVES):
        for t in range(ROW_DEV):
            for m in range(blocks):
                at, to = rows + t * blocks + m, (half * blocks + m) * P_SIZE
                right[t : t + 1, to : to + P_SIZE] = sums[half][at : at + 1]


def on_device(left_proj, right_proj, pair_cotangent, out_weight, out_bias):
    planes = lax.axis_size("plane")
    seq = lax.axis_size("seq")
    res = HALVES * planes
    scale = 1.0 / (SEQ_DEV * seq)
    rows = C * C // res
    columns = res * ROW_DEV
    left_rows = left_proj.reshape(ROW_DEV, SEQ_DEV, C)
    weight = out_weight.reshape(C, C, P_SIZE)

    opening = pl.pallas_call(
        opening_kernel,
        out_shape=jax.ShapeDtypeStruct((res, ROW_DEV, WIDE + P_SIZE), jnp.bfloat16),
        in_specs=[WHOLE] * 2,
        out_specs=WHOLE,
    )(right_proj, pair_cotangent)
    arrived = lax.all_to_all(opening, ("half", "plane"), 0, 0, tiled=True)
    right_all = arrived[:, :, :WIDE].reshape(columns, WIDE)

    mixed = dot32("isx,xyk->isyk", left_rows, weight)
    high = lax.reduce_precision(mixed, 8, 7)
    mixed_hi, mixed_lo = high.astype(jnp.bfloat16), (mixed - high).astype(jnp.bfloat16)
    back = (ROW_DEV, WIDE, P_SIZE)
    mixed_hi, mixed_lo = mixed_hi.reshape(back), mixed_lo.reshape(back)
    half_wide = jax.ShapeDtypeStruct((columns, WIDE // HALVES), jnp.float32)
    kept, sent = pl.pallas_call(
        right_kernel,
        out_shape=(half_wide, half_wide),
        in_specs=[pl.BlockSpec(memory_space=pltpu.SMEM)] + [WHOLE] * 3,
        out_specs=(WHOLE,) * 2,
        compiler_params=pltpu.CompilerParams(vmem_limit_bytes=16 * 1024 * 1024),
        cost_estimate=pl.CostEstimate(flops=150_000_000, bytes_accessed=1_000_000, transcendentals=0),
    )(lax.axis_index("half").reshape(1), pair_cotangent, mixed_hi, mixed_lo)
    got = lax.ppermute(sent, "half", [(0, 1), (1, 0)])
    grad_right = pl.pallas_call(
        packing_kernel,
        out_shape=jax.ShapeDtypeStruct((columns * WIDE // HALVES // P_SIZE, P_SIZE), jnp.float32),
        in_specs=[WHOLE] * 2,
        out_specs=WHOLE,
        scratch_shapes=[pltpu.VMEM((WIDE // HALVES // P_SIZE, columns, P_SIZE), jnp.float32)],
        compiler_params=pltpu.CompilerParams(vmem_limit_bytes=16 * 1024 * 1024),
        cost_estimate=pl.CostEstimate(flops=100_000, bytes_accessed=1_000_000, transcendentals=0),
    )(kept, got)
    left_cols = jnp.broadcast_to(left_rows.transpose(2, 0, 1)[:, :, None], (C, ROW_DEV, 2, SEQ_DEV))
    left_cols = left_cols.reshape(C, ROW_DEV * 2 * SEQ_DEV)

    message, terms = pl.pallas_call(
        products_kernel,
        out_shape=(
            jax.ShapeDtypeStruct((planes, 3 * rows, P_SIZE), jnp.bfloat16),
            jax.ShapeDtypeStruct(back, jnp.float32),
        ),
        in_specs=[WHOLE] * 4,
        out_specs=(WHOLE,) * 2,
        scratch_shapes=[pltpu.VMEM((C * C, P_SIZE), jnp.float32)],
        compiler_params=pltpu.CompilerParams(vmem_limit_bytes=16 * 1024 * 1024),
        cost_estimate=pl.CostEstimate(flops=200_000_000, bytes_accessed=2_000_000, transcendentals=0),
    )(right_all, pair_cotangent, left_cols, grad_right)

    parts = lax.all_to_all(message, "plane", 0, 0, tiled=True)

    pair, back_hi, back_lo = pl.pallas_call(
        pair_kernel,
        out_shape=(
            jax.ShapeDtypeStruct((ROW_DEV, columns, P_SIZE), jnp.float32),
            jax.ShapeDtypeStruct(back, jnp.bfloat16),
            jax.ShapeDtypeStruct(back, jnp.bfloat16),
        ),
        in_specs=[WHOLE] * 4,
        out_specs=(WHOLE,) * 3,
        compiler_params=pltpu.CompilerParams(vmem_limit_bytes=16 * 1024 * 1024),
        cost_estimate=pl.CostEstimate(flops=150_000_000, bytes_accessed=2_000_000, transcendentals=0),
    )(right_all, mixed_hi, mixed_lo, terms)
    cols = columns // seq
    here = lax.axis_index("seq")

    def columns_of(owner):
        return lax.dynamic_slice_in_dim(pair, owner * cols, cols, 1)

    others = []
    for step in range(1, seq):
        sent = columns_of(lax.bitwise_xor(here, jnp.int32(step)))
        others.append(lax.ppermute(sent, "seq", [(q, q ^ step) for q in range(seq)]))

    parts, arrived, back_hi, back_lo, pair_sum = lax.optimization_barrier(
        (parts, arrived, back_hi, back_lo, columns_of(here))
    )
    last = pl.pallas_call(
        middle_kernel,
        out_shape=jax.ShapeDtypeStruct((HALVES * seq, 2 * rows, P_SIZE), jnp.float32),
        in_specs=[pl.BlockSpec(memory_space=pltpu.SMEM), WHOLE],
        out_specs=WHOLE,
        compiler_params=pltpu.CompilerParams(vmem_limit_bytes=8 * 1024 * 1024),
    )(here.reshape(1), parts)
    last = lax.all_to_all(last, ("half", "seq"), 0, 0, tiled=True)
    grad_weight, grad_right = pl.pallas_call(
        lambda *refs: closing_kernel(scale, *refs),
        out_shape=(
            jax.ShapeDtypeStruct((rows, P_SIZE), jnp.float32),
            jax.ShapeDtypeStruct((ROW_DEV, WIDE), jnp.float32),
        ),
        in_specs=[WHOLE],
        out_specs=(WHOLE,) * 2,
        compiler_params=pltpu.CompilerParams(vmem_limit_bytes=8 * 1024 * 1024),
    )(last)
    for other in others:
        pair_sum = pair_sum + other
    pair_update = (pair_sum * scale + out_bias).astype(jnp.bfloat16)
    back_hi, back_lo = (term.reshape(ROW_DEV, SEQ_DEV, C, P_SIZE) for term in (back_hi, back_lo))
    grad_left = dot32("isyk,xyk->isx", back_hi, weight) + dot32("isyk,xyk->isx", back_lo, weight)
    grad_bias = jnp.sum(arrived[:, :, WIDE:], axis=(0, 1), dtype=jnp.float32)
    return pair_update, (grad_left * scale).reshape(ROW_DEV, WIDE), grad_right, grad_weight, grad_bias


def solution(mesh):
    res, seq = mesh.devices.shape
    fine = Mesh(mesh.devices.reshape(HALVES, res // HALVES, seq), ("half", "plane", "seq"))
    across = ("half", "plane")
    return jax.shard_map(
        on_device,
        mesh=fine,
        in_specs=(P(across, "seq"), P(across, "seq"), P(across, None, None), P(), P()),
        out_specs=(P(across, "seq", None), P(across, "seq"), P(across, "seq"), P(across, None), P()),
        check_vma=False,
    )
```

```python
import jax
import jax.numpy as jnp
from jax import lax
from jax.experimental import pallas as pl
from jax.experimental.pallas import tpu as pltpu
from jax.sharding import Mesh
from jax.sharding import PartitionSpec as P

C = 32
P_SIZE = 128
SEQ_DEV = 16
ROW_DEV = 2
WIDE = SEQ_DEV * C
HALVES = 2
WHOLE = pl.BlockSpec(memory_space=pltpu.VMEM)


def split_in_two(value):
    high = value.astype(jnp.bfloat16)
    return high, (value - high.astype(jnp.float32)).astype(jnp.bfloat16)


def dot32(form, a, b):
    return jnp.einsum(form, a, b, preferred_element_type=jnp.float32)


def opening_kernel(right, out):
    out[...] = jnp.broadcast_to(right[...][None], out.shape)


def right_kernel(place, cotan, mixed_hi, mixed_lo, kept, sent):
    total = jnp.zeros((cotan.shape[1], WIDE), jnp.float32)
    for i in range(ROW_DEV):
        for mixed in (mixed_hi, mixed_lo):
            total += lax.dot_general(cotan[i], mixed[i], (((1,), (1,)), ((), ())), preferred_element_type=jnp.float32)
    low, high = total[:, : WIDE // 2], total[:, WIDE // 2 :]
    kept[...] = jnp.where(place[0] == 0, low, high)
    sent[...] = jnp.where(place[0] == 0, high, low).astype(jnp.bfloat16)


def packing_kernel(kept, got, out, total):
    blocks = kept.shape[1] // P_SIZE
    lines = ROW_DEV * blocks * HALVES
    planes = out.shape[0] // lines
    for m in range(blocks):
        cut = slice(m * P_SIZE, (m + 1) * P_SIZE)
        total[m] = kept[:, cut] + got[:, cut].astype(jnp.float32)
        for half in range(HALVES):
            for t in range(ROW_DEV):
                out[pl.ds((half * ROW_DEV + t) * blocks + m, planes, stride=lines), :] = total[
                    m, pl.ds(half * planes * ROW_DEV + t, planes, stride=ROW_DEV), :
                ]


def products_kernel(right, cotan, left_cols, grad_right, message, back, weight):
    rows = right[...]
    both = jnp.concatenate([cotan[0], cotan[1]], axis=1)
    terms = lax.dot_general(rows, both, (((0,), (0,)), ((), ())), preferred_element_type=jnp.float32)
    back[0] = terms[:, :P_SIZE]
    back[1] = terms[:, P_SIZE:]
    lhs = left_cols[...]
    for y in range(C):
        parts = []
        for i in range(ROW_DEV):
            parts += split_in_two(back[i, pl.ds(y, SEQ_DEV, stride=C), :])
        weight[pl.ds(y, C, stride=C), :] = jnp.dot(
            lhs, jnp.concatenate(parts, axis=0), preferred_element_type=jnp.float32
        )
    planes = message.shape[0]
    halves = weight[...].reshape(HALVES, planes, C * C // (HALVES * planes), P_SIZE)
    own = grad_right[...].reshape(planes, grad_right.shape[0] // planes, P_SIZE)
    total = jnp.sum(both.astype(jnp.float32), axis=0, keepdims=True)
    total = total[:, :P_SIZE] + total[:, P_SIZE:]
    high = total.astype(jnp.bfloat16).astype(jnp.float32)
    line = lax.broadcasted_iota(jnp.int32, halves.shape[2:], 0)
    bias = jnp.where(line == 0, high, jnp.where(line == 1, total - high, 0.0))
    bias = jnp.broadcast_to(bias[None], halves.shape[1:])
    message[...] = jnp.concatenate([halves[0], halves[1], own, bias], axis=1).astype(jnp.bfloat16)


def pair_kernel(right, mixed_hi, mixed_lo, back, pair, back_hi, back_lo):
    rows = right[...]
    for i in range(ROW_DEV):
        pair[i] = jnp.dot(rows, mixed_hi[i], preferred_element_type=jnp.float32) + jnp.dot(
            rows, mixed_lo[i], preferred_element_type=jnp.float32
        )
        back_hi[i], back_lo[i] = split_in_two(back[i])


def middle_kernel(place, parts, out):
    total = jnp.sum(parts[...].astype(jnp.float32), axis=0)
    rows = total.shape[0] // 4
    seq = out.shape[0] // HALVES
    right, bias = total[2 * rows : 3 * rows], total[3 * rows : 3 * rows + rows // 2]
    rights = [right[: rows // 2], right[rows // 2 :]]
    for half in range(HALVES):
        mine = total[half * rows : (half + 1) * rows]
        for q in range(seq):
            out[half * seq + q, :rows] = mine
            mine_too = jnp.where(place[0] == q, rights[half], 0.0)
            out[half * seq + q, rows:] = jnp.concatenate([mine_too, bias], axis=0)


def closing_kernel(scale, parts, weight, right, bias):
    rows = weight.shape[0]
    seq = parts.shape[0] // HALVES
    sums = [jnp.sum(parts[half * seq : (half + 1) * seq], axis=0) * scale for half in range(HALVES)]
    weight[...] = sums[0][:rows] + sums[1][:rows]
    pieces = (sums[0] + sums[1])[rows + rows // 2 :]
    bias[...] = (pieces[0:1] + pieces[1:2]) * (1.0 / (scale * seq))
    blocks = WIDE // HALVES // P_SIZE
    for half in range(HALVES):
        for t in range(ROW_DEV):
            for m in range(blocks):
                at, to = rows + t * blocks + m, (half * blocks + m) * P_SIZE
                right[t : t + 1, to : to + P_SIZE] = sums[half][at : at + 1]


def on_device(left_proj, right_proj, pair_cotangent, out_weight, out_bias):
    planes = lax.axis_size("plane")
    seq = lax.axis_size("seq")
    res = HALVES * planes
    scale = 1.0 / (SEQ_DEV * seq)
    rows = C * C // res
    columns = res * ROW_DEV
    left_rows = left_proj.reshape(ROW_DEV, SEQ_DEV, C)
    weight = out_weight.reshape(C, C, P_SIZE)

    opening = pl.pallas_call(
        opening_kernel,
        out_shape=jax.ShapeDtypeStruct((res, ROW_DEV, WIDE), jnp.bfloat16),
        in_specs=[WHOLE],
        out_specs=WHOLE,
    )(right_proj)
    arrived = lax.all_to_all(opening, ("half", "plane"), 0, 0, tiled=True)
    right_all = arrived.reshape(columns, WIDE)

    mixed = dot32("isx,xyk->isyk", left_rows, weight)
    high = lax.reduce_precision(mixed, 8, 7)
    mixed_hi, mixed_lo = high.astype(jnp.bfloat16), (mixed - high).astype(jnp.bfloat16)
    back = (ROW_DEV, WIDE, P_SIZE)
    mixed_hi, mixed_lo = mixed_hi.reshape(back), mixed_lo.reshape(back)
    half_wide = jax.ShapeDtypeStruct((columns, WIDE // HALVES), jnp.float32)
    kept, sent = pl.pallas_call(
        right_kernel,
        out_shape=(half_wide, jax.ShapeDtypeStruct(half_wide.shape, jnp.bfloat16)),
        in_specs=[pl.BlockSpec(memory_space=pltpu.SMEM)] + [WHOLE] * 3,
        out_specs=(WHOLE,) * 2,
        compiler_params=pltpu.CompilerParams(vmem_limit_bytes=16 * 1024 * 1024),
        cost_estimate=pl.CostEstimate(flops=150_000_000, bytes_accessed=1_000_000, transcendentals=0),
    )(lax.axis_index("half").reshape(1), pair_cotangent, mixed_hi, mixed_lo)
    got = lax.ppermute(sent, "half", [(0, 1), (1, 0)])
    grad_right = pl.pallas_call(
        packing_kernel,
        out_shape=jax.ShapeDtypeStruct((columns * WIDE // HALVES // P_SIZE, P_SIZE), jnp.float32),
        in_specs=[WHOLE] * 2,
        out_specs=WHOLE,
        scratch_shapes=[pltpu.VMEM((WIDE // HALVES // P_SIZE, columns, P_SIZE), jnp.float32)],
        compiler_params=pltpu.CompilerParams(vmem_limit_bytes=16 * 1024 * 1024),
        cost_estimate=pl.CostEstimate(flops=100_000, bytes_accessed=1_000_000, transcendentals=0),
    )(kept, got)
    left_cols = jnp.broadcast_to(left_rows.transpose(2, 0, 1)[:, :, None], (C, ROW_DEV, 2, SEQ_DEV))
    left_cols = left_cols.reshape(C, ROW_DEV * 2 * SEQ_DEV)

    message, terms = pl.pallas_call(
        products_kernel,
        out_shape=(
            jax.ShapeDtypeStruct((planes, 4 * rows, P_SIZE), jnp.bfloat16),
            jax.ShapeDtypeStruct(back, jnp.float32),
        ),
        in_specs=[WHOLE] * 4,
        out_specs=(WHOLE,) * 2,
        scratch_shapes=[pltpu.VMEM((C * C, P_SIZE), jnp.float32)],
        compiler_params=pltpu.CompilerParams(vmem_limit_bytes=16 * 1024 * 1024),
        cost_estimate=pl.CostEstimate(flops=200_000_000, bytes_accessed=2_000_000, transcendentals=0),
    )(right_all, pair_cotangent, left_cols, grad_right)

    parts = lax.all_to_all(message, "plane", 0, 0, tiled=True)

    pair, back_hi, back_lo = pl.pallas_call(
        pair_kernel,
        out_shape=(
            jax.ShapeDtypeStruct((ROW_DEV, columns, P_SIZE), jnp.float32),
            jax.ShapeDtypeStruct(back, jnp.bfloat16),
            jax.ShapeDtypeStruct(back, jnp.bfloat16),
        ),
        in_specs=[WHOLE] * 4,
        out_specs=(WHOLE,) * 3,
        compiler_params=pltpu.CompilerParams(vmem_limit_bytes=16 * 1024 * 1024),
        cost_estimate=pl.CostEstimate(flops=150_000_000, bytes_accessed=2_000_000, transcendentals=0),
    )(right_all, mixed_hi, mixed_lo, terms)
    cols = columns // seq
    here = lax.axis_index("seq")

    def columns_of(owner):
        return lax.dynamic_slice_in_dim(pair, owner * cols, cols, 1)

    others = []
    for step in range(1, seq):
        sent = columns_of(lax.bitwise_xor(here, jnp.int32(step)))
        others.append(lax.ppermute(sent, "seq", [(q, q ^ step) for q in range(seq)]))

    parts, back_hi, back_lo, pair_sum = lax.optimization_barrier((parts, back_hi, back_lo, columns_of(here)))
    last = pl.pallas_call(
        middle_kernel,
        out_shape=jax.ShapeDtypeStruct((HALVES * seq, 2 * rows, P_SIZE), jnp.float32),
        in_specs=[pl.BlockSpec(memory_space=pltpu.SMEM), WHOLE],
        out_specs=WHOLE,
        compiler_params=pltpu.CompilerParams(vmem_limit_bytes=8 * 1024 * 1024),
    )(here.reshape(1), parts)
    last = lax.all_to_all(last, ("half", "seq"), 0, 0, tiled=True)
    grad_weight, grad_right, grad_bias = pl.pallas_call(
        lambda *refs: closing_kernel(scale, *refs),
        out_shape=(
            jax.ShapeDtypeStruct((rows, P_SIZE), jnp.float32),
            jax.ShapeDtypeStruct((ROW_DEV, WIDE), jnp.float32),
            jax.ShapeDtypeStruct((1, P_SIZE), jnp.float32),
        ),
        in_specs=[WHOLE],
        out_specs=(WHOLE,) * 3,
        compiler_params=pltpu.CompilerParams(vmem_limit_bytes=8 * 1024 * 1024),
    )(last)
    for other in others:
        pair_sum = pair_sum + other
    pair_update = (pair_sum * scale + out_bias).astype(jnp.bfloat16)
    back_hi, back_lo = (term.reshape(ROW_DEV, SEQ_DEV, C, P_SIZE) for term in (back_hi, back_lo))
    grad_left = dot32("isyk,xyk->isx", back_hi, weight) + dot32("isyk,xyk->isx", back_lo, weight)
    return pair_update, (grad_left * scale).reshape(ROW_DEV, WIDE), grad_right, grad_weight, grad_bias[0]


def solution(mesh):
    res, seq = mesh.devices.shape
    fine = Mesh(mesh.devices.reshape(HALVES, res // HALVES, seq), ("half", "plane", "seq"))
    across = ("half", "plane")
    return jax.shard_map(
        on_device,
        mesh=fine,
        in_specs=(P(across, "seq"), P(across, "seq"), P(across, None, None), P(), P()),
        out_specs=(P(across, "seq", None), P(across, "seq"), P(across, "seq"), P(across, None), P()),
        check_vma=False,
    )
```

```python
import jax
import jax.numpy as jnp
from jax import lax
from jax.experimental import pallas as pl
from jax.experimental.pallas import tpu as pltpu
from jax.sharding import Mesh
from jax.sharding import PartitionSpec as P

C = 32
P_SIZE = 128
SEQ_DEV = 16
ROW_DEV = 2
WIDE = SEQ_DEV * C
HALVES = 2
WHOLE = pl.BlockSpec(memory_space=pltpu.VMEM)


def split_in_two(value):
    high = value.astype(jnp.bfloat16)
    return high, (value - high.astype(jnp.float32)).astype(jnp.bfloat16)


def dot32(form, a, b):
    return jnp.einsum(form, a, b, preferred_element_type=jnp.float32)


def opening_kernel(right, out, block, done):
    block[...] = jnp.broadcast_to(right[...][None], block.shape)
    size = block.shape[0]
    copies = [
        pltpu.make_async_copy(block, out.at[pl.ds(size * n, size)], done.at[n]) for n in range(out.shape[0] // size)
    ]
    for copy in copies:
        copy.start()
    for copy in copies:
        copy.wait()


def right_kernel(place, cotan, mixed_hi, mixed_lo, kept, sent):
    total = jnp.zeros((cotan.shape[1], WIDE), jnp.float32)
    for i in range(ROW_DEV):
        for mixed in (mixed_hi, mixed_lo):
            total += lax.dot_general(cotan[i], mixed[i], (((1,), (1,)), ((), ())), preferred_element_type=jnp.float32)
    low, high = total[:, : WIDE // 2], total[:, WIDE // 2 :]
    kept[...] = jnp.where(place[0] == 0, low, high)
    sent[...] = jnp.where(place[0] == 0, high, low).astype(jnp.bfloat16)


def packing_kernel(kept, got, out, total):
    blocks = kept.shape[1] // P_SIZE
    lines = ROW_DEV * blocks * HALVES
    planes = out.shape[0] // lines
    for m in range(blocks):
        cut = slice(m * P_SIZE, (m + 1) * P_SIZE)
        total[m] = kept[:, cut] + got[:, cut].astype(jnp.float32)
        for half in range(HALVES):
            for t in range(ROW_DEV):
                out[pl.ds((half * ROW_DEV + t) * blocks + m, planes, stride=lines), :] = total[
                    m, pl.ds(half * planes * ROW_DEV + t, planes, stride=ROW_DEV), :
                ]


def products_kernel(right, cotan, left_cols, grad_right, message, back, weight, own, other, done):
    both = jnp.concatenate([cotan[0], cotan[1]], axis=1)
    planes, lines = own.shape[0], own.shape[1] // 2
    total = jnp.sum(both.astype(jnp.float32), axis=0, keepdims=True)
    total = total[:, :P_SIZE] + total[:, P_SIZE:]
    high = total.astype(jnp.bfloat16).astype(jnp.float32)
    line = lax.broadcasted_iota(jnp.int32, (lines, P_SIZE), 0)
    bias = jnp.where(line == 0, high, jnp.where(line == 1, total - high, 0.0))
    bias = jnp.broadcast_to(bias[None], (planes, lines, P_SIZE))
    other[...] = jnp.concatenate([grad_right[...].reshape(planes, lines, P_SIZE), bias], axis=1).astype(jnp.bfloat16)
    first = pltpu.make_async_copy(other, message.at[:, pl.ds(2 * lines, 2 * lines)], done.at[0])
    first.start()

    terms = lax.dot_general(right[...], both, (((0,), (0,)), ((), ())), preferred_element_type=jnp.float32)
    back[0] = terms[:, :P_SIZE]
    back[1] = terms[:, P_SIZE:]
    lhs = left_cols[...]
    group = 8
    for y0 in range(0, C, group):
        columns = []
        for y in range(y0, y0 + group):
            parts = []
            for i in range(ROW_DEV):
                parts += split_in_two(back[i, pl.ds(y, SEQ_DEV, stride=C), :])
            columns.append(jnp.concatenate(parts, axis=0))
        terms = jnp.dot(lhs, jnp.concatenate(columns, axis=1), preferred_element_type=jnp.float32)
        for n in range(group):
            weight[pl.ds(y0 + n, C, stride=C), :] = terms[:, n * P_SIZE : (n + 1) * P_SIZE]
    halves = weight[...].reshape(HALVES, planes, lines, P_SIZE)
    own[...] = jnp.concatenate([halves[0], halves[1]], axis=1).astype(jnp.bfloat16)
    second = pltpu.make_async_copy(own, message.at[:, pl.ds(0, 2 * lines)], done.at[1])
    second.start()
    first.wait()
    second.wait()


def pair_kernel(right, mixed_hi, mixed_lo, back, pair, back_hi, back_lo):
    rows = right[...]
    for i in range(ROW_DEV):
        pair[i] = jnp.dot(rows, mixed_hi[i], preferred_element_type=jnp.float32) + jnp.dot(
            rows, mixed_lo[i], preferred_element_type=jnp.float32
        )
        back_hi[i], back_lo[i] = split_in_two(back[i])


def middle_kernel(place, parts, out):
    total = jnp.sum(parts[...].astype(jnp.float32), axis=0)
    rows = total.shape[0] // 4
    seq = out.shape[0] // HALVES
    right, bias = total[2 * rows : 3 * rows], total[3 * rows : 3 * rows + rows // 2]
    rights = [right[: rows // 2], right[rows // 2 :]]
    for half in range(HALVES):
        mine = total[half * rows : (half + 1) * rows]
        for q in range(seq):
            out[half * seq + q, :rows] = mine
            mine_too = jnp.where(place[0] == q, rights[half], 0.0)
            out[half * seq + q, rows:] = jnp.concatenate([mine_too, bias], axis=0)


def closing_kernel(scale, parts, weight, right, bias):
    rows = weight.shape[0]
    seq = parts.shape[0] // HALVES
    sums = [jnp.sum(parts[half * seq : (half + 1) * seq], axis=0) * scale for half in range(HALVES)]
    weight[...] = sums[0][:rows] + sums[1][:rows]
    pieces = (sums[0] + sums[1])[rows + rows // 2 :]
    bias[...] = (pieces[0:1] + pieces[1:2]) * (1.0 / (scale * seq))
    blocks = WIDE // HALVES // P_SIZE
    for half in range(HALVES):
        for t in range(ROW_DEV):
            for m in range(blocks):
                at, to = rows + t * blocks + m, (half * blocks + m) * P_SIZE
                right[t : t + 1, to : to + P_SIZE] = sums[half][at : at + 1]


def on_device(left_proj, right_proj, pair_cotangent, out_weight, out_bias):
    planes = lax.axis_size("plane")
    seq = lax.axis_size("seq")
    res = HALVES * planes
    scale = 1.0 / (SEQ_DEV * seq)
    rows = C * C // res
    columns = res * ROW_DEV
    left_rows = left_proj.reshape(ROW_DEV, SEQ_DEV, C)
    weight = out_weight.reshape(C, C, P_SIZE)

    opening = pl.pallas_call(
        opening_kernel,
        out_shape=jax.ShapeDtypeStruct((res, ROW_DEV, WIDE), jnp.bfloat16),
        in_specs=[WHOLE],
        out_specs=pl.BlockSpec(memory_space=pl.ANY),
        scratch_shapes=[pltpu.VMEM((16, ROW_DEV, WIDE), jnp.bfloat16), pltpu.SemaphoreType.DMA((res // 16,))],
    )(right_proj)
    arrived = lax.all_to_all(opening, ("half", "plane"), 0, 0, tiled=True)
    right_all = arrived.reshape(columns, WIDE)

    mixed = dot32("isx,xyk->isyk", left_rows, weight)
    high = lax.reduce_precision(mixed, 8, 7)
    mixed_hi, mixed_lo = high.astype(jnp.bfloat16), (mixed - high).astype(jnp.bfloat16)
    back = (ROW_DEV, WIDE, P_SIZE)
    mixed_hi, mixed_lo = mixed_hi.reshape(back), mixed_lo.reshape(back)
    half_wide = jax.ShapeDtypeStruct((columns, WIDE // HALVES), jnp.float32)
    kept, sent = pl.pallas_call(
        right_kernel,
        out_shape=(half_wide, jax.ShapeDtypeStruct(half_wide.shape, jnp.bfloat16)),
        in_specs=[pl.BlockSpec(memory_space=pltpu.SMEM)] + [WHOLE] * 3,
        out_specs=(WHOLE,) * 2,
        compiler_params=pltpu.CompilerParams(vmem_limit_bytes=16 * 1024 * 1024),
        cost_estimate=pl.CostEstimate(flops=150_000_000, bytes_accessed=1_000_000, transcendentals=0),
    )(lax.axis_index("half").reshape(1), pair_cotangent, mixed_hi, mixed_lo)
    got = lax.ppermute(sent, "half", [(0, 1), (1, 0)])
    grad_right = pl.pallas_call(
        packing_kernel,
        out_shape=jax.ShapeDtypeStruct((columns * WIDE // HALVES // P_SIZE, P_SIZE), jnp.float32),
        in_specs=[WHOLE] * 2,
        out_specs=WHOLE,
        scratch_shapes=[pltpu.VMEM((WIDE // HALVES // P_SIZE, columns, P_SIZE), jnp.float32)],
        compiler_params=pltpu.CompilerParams(vmem_limit_bytes=16 * 1024 * 1024),
        cost_estimate=pl.CostEstimate(flops=100_000, bytes_accessed=1_000_000, transcendentals=0),
    )(kept, got)
    left_cols = jnp.broadcast_to(left_rows.transpose(2, 0, 1)[:, :, None], (C, ROW_DEV, 2, SEQ_DEV))
    left_cols = left_cols.reshape(C, ROW_DEV * 2 * SEQ_DEV)

    message, terms = pl.pallas_call(
        products_kernel,
        out_shape=(
            jax.ShapeDtypeStruct((planes, 4 * rows, P_SIZE), jnp.bfloat16),
            jax.ShapeDtypeStruct(back, jnp.float32),
        ),
        in_specs=[WHOLE] * 4,
        out_specs=(pl.BlockSpec(memory_space=pl.ANY), WHOLE),
        scratch_shapes=[
            pltpu.VMEM((C * C, P_SIZE), jnp.float32),
            pltpu.VMEM((planes, 2 * rows, P_SIZE), jnp.bfloat16),
            pltpu.VMEM((planes, 2 * rows, P_SIZE), jnp.bfloat16),
            pltpu.SemaphoreType.DMA((2,)),
        ],
        compiler_params=pltpu.CompilerParams(vmem_limit_bytes=16 * 1024 * 1024),
        cost_estimate=pl.CostEstimate(flops=200_000_000, bytes_accessed=2_000_000, transcendentals=0),
    )(right_all, pair_cotangent, left_cols, grad_right)

    parts = lax.all_to_all(message, "plane", 0, 0, tiled=True)

    pair, back_hi, back_lo = pl.pallas_call(
        pair_kernel,
        out_shape=(
            jax.ShapeDtypeStruct((ROW_DEV, columns, P_SIZE), jnp.float32),
            jax.ShapeDtypeStruct(back, jnp.bfloat16),
            jax.ShapeDtypeStruct(back, jnp.bfloat16),
        ),
        in_specs=[WHOLE] * 4,
        out_specs=(WHOLE,) * 3,
        compiler_params=pltpu.CompilerParams(vmem_limit_bytes=16 * 1024 * 1024),
        cost_estimate=pl.CostEstimate(flops=150_000_000, bytes_accessed=2_000_000, transcendentals=0),
    )(right_all, mixed_hi, mixed_lo, terms)
    cols = columns // seq
    here = lax.axis_index("seq")

    def columns_of(owner):
        return lax.dynamic_slice_in_dim(pair, owner * cols, cols, 1)

    pair_sum = columns_of(here)
    for step in range(1, seq):
        sent = columns_of(lax.bitwise_xor(here, jnp.int32(step)))
        pair_sum = pair_sum + lax.ppermute(sent, "seq", [(q, q ^ step) for q in range(seq)])
    pair_update = (pair_sum * scale + out_bias).astype(jnp.bfloat16)
    back_hi, back_lo = (term.reshape(ROW_DEV, SEQ_DEV, C, P_SIZE) for term in (back_hi, back_lo))
    grad_left = dot32("isyk,xyk->isx", back_hi, weight) + dot32("isyk,xyk->isx", back_lo, weight)
    grad_left = (grad_left * scale).reshape(ROW_DEV, WIDE)

    parts, pair_update, grad_left = lax.optimization_barrier((parts, pair_update, grad_left))
    last = pl.pallas_call(
        middle_kernel,
        out_shape=jax.ShapeDtypeStruct((HALVES * seq, 2 * rows, P_SIZE), jnp.float32),
        in_specs=[pl.BlockSpec(memory_space=pltpu.SMEM), WHOLE],
        out_specs=WHOLE,
        compiler_params=pltpu.CompilerParams(vmem_limit_bytes=8 * 1024 * 1024),
    )(here.reshape(1), parts)
    last = lax.all_to_all(last, ("half", "seq"), 0, 0, tiled=True)
    grad_weight, grad_right, grad_bias = pl.pallas_call(
        lambda *refs: closing_kernel(scale, *refs),
        out_shape=(
            jax.ShapeDtypeStruct((rows, P_SIZE), jnp.float32),
            jax.ShapeDtypeStruct((ROW_DEV, WIDE), jnp.float32),
            jax.ShapeDtypeStruct((1, P_SIZE), jnp.float32),
        ),
        in_specs=[WHOLE],
        out_specs=(WHOLE,) * 3,
        compiler_params=pltpu.CompilerParams(vmem_limit_bytes=8 * 1024 * 1024),
    )(last)
    return pair_update, grad_left, grad_right, grad_weight, grad_bias[0]


def solution(mesh):
    res, seq = mesh.devices.shape
    fine = Mesh(mesh.devices.reshape(HALVES, res // HALVES, seq), ("half", "plane", "seq"))
    across = ("half", "plane")
    return jax.shard_map(
        on_device,
        mesh=fine,
        in_specs=(P(across, "seq"), P(across, "seq"), P(across, None, None), P(), P()),
        out_specs=(P(across, "seq", None), P(across, "seq"), P(across, "seq"), P(across, None), P()),
        check_vma=False,
    )
```

```python
import jax
import jax.numpy as jnp
from jax import lax
from jax.experimental import pallas as pl
from jax.experimental.pallas import tpu as pltpu
from jax.sharding import Mesh
from jax.sharding import PartitionSpec as P

C = 32
P_SIZE = 128
SEQ_DEV = 16
ROW_DEV = 2
WIDE = SEQ_DEV * C
HALVES = 2
SIDE = 8
WHOLE = pl.BlockSpec(memory_space=pltpu.VMEM)


def split_in_two(value):
    high = value.astype(jnp.bfloat16)
    return high, (value - high.astype(jnp.float32)).astype(jnp.bfloat16)


def dot32(form, a, b):
    return jnp.einsum(form, a, b, preferred_element_type=jnp.float32)


def opening_kernel(right, out, block, done):
    block[...] = jnp.broadcast_to(right[...][None], block.shape)
    size = block.shape[0]
    copies = [
        pltpu.make_async_copy(block, out.at[pl.ds(size * n, size)], done.at[n]) for n in range(out.shape[0] // size)
    ]
    for copy in copies:
        copy.start()
    for copy in copies:
        copy.wait()


def right_kernel(place, cotan, mixed_hi, mixed_lo, kept, sent):
    total = jnp.zeros((cotan.shape[1], WIDE), jnp.float32)
    for i in range(ROW_DEV):
        for mixed in (mixed_hi, mixed_lo):
            total += lax.dot_general(cotan[i], mixed[i], (((1,), (1,)), ((), ())), preferred_element_type=jnp.float32)
    low, high = total[:, : WIDE // 2], total[:, WIDE // 2 :]
    kept[...] = jnp.where(place[0] == 0, low, high)
    sent[...] = jnp.where(place[0] == 0, high, low).astype(jnp.bfloat16)


def packing_kernel(kept, got, out, total):
    blocks = kept.shape[1] // P_SIZE
    lines = ROW_DEV * blocks * HALVES
    planes = out.shape[0] // lines
    for m in range(blocks):
        cut = slice(m * P_SIZE, (m + 1) * P_SIZE)
        total[m] = kept[:, cut] + got[:, cut].astype(jnp.float32)
        for half in range(HALVES):
            for t in range(ROW_DEV):
                out[pl.ds((half * ROW_DEV + t) * blocks + m, planes, stride=lines), :] = total[
                    m, pl.ds(half * planes * ROW_DEV + t, planes, stride=ROW_DEV), :
                ]


def products_kernel(right, cotan, left_cols, grad_right, message, back, weight, own, other, done):
    both = jnp.concatenate([cotan[0], cotan[1]], axis=1)
    planes, lines = SIDE * SIDE, own.shape[2] // 2
    total = jnp.sum(both.astype(jnp.float32), axis=0, keepdims=True)
    total = total[:, :P_SIZE] + total[:, P_SIZE:]
    high = total.astype(jnp.bfloat16).astype(jnp.float32)
    line = lax.broadcasted_iota(jnp.int32, (lines, P_SIZE), 0)
    bias = jnp.where(line == 0, high, jnp.where(line == 1, total - high, 0.0))
    bias = jnp.broadcast_to(bias[None], (planes, lines, P_SIZE))
    tiles = jnp.concatenate([grad_right[...].reshape(planes, lines, P_SIZE), bias], axis=1).astype(jnp.bfloat16)
    for z in range(SIDE):
        other[:, z] = tiles[z * SIDE : (z + 1) * SIDE]
    first = pltpu.make_async_copy(other, message.at[:, :, pl.ds(2 * lines, 2 * lines)], done.at[0])
    first.start()

    terms = lax.dot_general(right[...], both, (((0,), (0,)), ((), ())), preferred_element_type=jnp.float32)
    back[0] = terms[:, :P_SIZE]
    back[1] = terms[:, P_SIZE:]
    lhs = left_cols[...]
    group = 8
    for y0 in range(0, C, group):
        columns = []
        for y in range(y0, y0 + group):
            parts = []
            for i in range(ROW_DEV):
                parts += split_in_two(back[i, pl.ds(y, SEQ_DEV, stride=C), :])
            columns.append(jnp.concatenate(parts, axis=0))
        terms = jnp.dot(lhs, jnp.concatenate(columns, axis=1), preferred_element_type=jnp.float32)
        for n in range(group):
            weight[pl.ds(y0 + n, C, stride=C), :] = terms[:, n * P_SIZE : (n + 1) * P_SIZE]
    halves = weight[...].reshape(HALVES, planes, lines, P_SIZE)
    tiles = jnp.concatenate([halves[0], halves[1]], axis=1).astype(jnp.bfloat16)
    for z in range(SIDE):
        own[:, z] = tiles[z * SIDE : (z + 1) * SIDE]
    second = pltpu.make_async_copy(own, message.at[:, :, pl.ds(0, 2 * lines)], done.at[1])
    second.start()
    first.wait()
    second.wait()


def pair_kernel(right, mixed_hi, mixed_lo, back, pair, back_hi, back_lo):
    rows = right[...]
    for i in range(ROW_DEV):
        pair[i] = jnp.dot(rows, mixed_hi[i], preferred_element_type=jnp.float32) + jnp.dot(
            rows, mixed_lo[i], preferred_element_type=jnp.float32
        )
        back_hi[i], back_lo[i] = split_in_two(back[i])


def middle_kernel(place, parts, out):
    total = jnp.sum(parts[...].astype(jnp.float32), axis=0)
    rows = total.shape[0] // 4
    seq = out.shape[0] // HALVES
    right, bias = total[2 * rows : 3 * rows], total[3 * rows : 3 * rows + rows // 2]
    rights = [right[: rows // 2], right[rows // 2 :]]
    for half in range(HALVES):
        mine = total[half * rows : (half + 1) * rows]
        for q in range(seq):
            out[half * seq + q, :rows] = mine
            mine_too = jnp.where(place[0] == q, rights[half], 0.0)
            out[half * seq + q, rows:] = jnp.concatenate([mine_too, bias], axis=0)


def closing_kernel(scale, parts, weight, right, bias):
    rows = weight.shape[0]
    seq = parts.shape[0] // HALVES
    sums = [jnp.sum(parts[half * seq : (half + 1) * seq], axis=0) * scale for half in range(HALVES)]
    weight[...] = sums[0][:rows] + sums[1][:rows]
    pieces = (sums[0] + sums[1])[rows + rows // 2 :]
    bias[...] = (pieces[0:1] + pieces[1:2]) * (1.0 / (scale * seq))
    blocks = WIDE // HALVES // P_SIZE
    for half in range(HALVES):
        for t in range(ROW_DEV):
            for m in range(blocks):
                at, to = rows + t * blocks + m, (half * blocks + m) * P_SIZE
                right[t : t + 1, to : to + P_SIZE] = sums[half][at : at + 1]


def on_device(left_proj, right_proj, pair_cotangent, out_weight, out_bias):
    planes = SIDE * SIDE
    seq = lax.axis_size("seq")
    res = HALVES * planes
    scale = 1.0 / (SEQ_DEV * seq)
    rows = C * C // res
    columns = res * ROW_DEV
    left_rows = left_proj.reshape(ROW_DEV, SEQ_DEV, C)
    weight = out_weight.reshape(C, C, P_SIZE)

    opening = pl.pallas_call(
        opening_kernel,
        out_shape=jax.ShapeDtypeStruct((res, ROW_DEV, WIDE), jnp.bfloat16),
        in_specs=[WHOLE],
        out_specs=pl.BlockSpec(memory_space=pl.ANY),
        scratch_shapes=[pltpu.VMEM((16, ROW_DEV, WIDE), jnp.bfloat16), pltpu.SemaphoreType.DMA((res // 16,))],
    )(right_proj)
    arrived = lax.all_to_all(opening, ("y", "z", "half"), 0, 0, tiled=True)
    cotan_arrived = pair_cotangent.reshape(ROW_DEV, HALVES, SIDE, SIDE, ROW_DEV, P_SIZE)
    cotan_arrived = cotan_arrived.transpose(0, 3, 2, 1, 4, 5).reshape(pair_cotangent.shape)

    mixed = dot32("isx,xyk->isyk", left_rows, weight)
    high = lax.reduce_precision(mixed, 8, 7)
    mixed_hi, mixed_lo = high.astype(jnp.bfloat16), (mixed - high).astype(jnp.bfloat16)
    back = (ROW_DEV, WIDE, P_SIZE)
    mixed_hi, mixed_lo = mixed_hi.reshape(back), mixed_lo.reshape(back)
    half_wide = jax.ShapeDtypeStruct((columns, WIDE // HALVES), jnp.float32)
    kept, sent = pl.pallas_call(
        right_kernel,
        out_shape=(half_wide, jax.ShapeDtypeStruct(half_wide.shape, jnp.bfloat16)),
        in_specs=[pl.BlockSpec(memory_space=pltpu.SMEM)] + [WHOLE] * 3,
        out_specs=(WHOLE,) * 2,
        compiler_params=pltpu.CompilerParams(vmem_limit_bytes=16 * 1024 * 1024),
        cost_estimate=pl.CostEstimate(flops=150_000_000, bytes_accessed=1_000_000, transcendentals=0),
    )(lax.axis_index("half").reshape(1), pair_cotangent, mixed_hi, mixed_lo)
    got = lax.ppermute(sent, "half", [(0, 1), (1, 0)])
    grad_right = pl.pallas_call(
        packing_kernel,
        out_shape=jax.ShapeDtypeStruct((columns * WIDE // HALVES // P_SIZE, P_SIZE), jnp.float32),
        in_specs=[WHOLE] * 2,
        out_specs=WHOLE,
        scratch_shapes=[pltpu.VMEM((WIDE // HALVES // P_SIZE, columns, P_SIZE), jnp.float32)],
        compiler_params=pltpu.CompilerParams(vmem_limit_bytes=16 * 1024 * 1024),
        cost_estimate=pl.CostEstimate(flops=100_000, bytes_accessed=1_000_000, transcendentals=0),
    )(kept, got)
    left_cols = jnp.broadcast_to(left_rows.transpose(2, 0, 1)[:, :, None], (C, ROW_DEV, 2, SEQ_DEV))
    left_cols = left_cols.reshape(C, ROW_DEV * 2 * SEQ_DEV)

    message, terms = pl.pallas_call(
        products_kernel,
        out_shape=(
            jax.ShapeDtypeStruct((SIDE, SIDE, 4 * rows, P_SIZE), jnp.bfloat16),
            jax.ShapeDtypeStruct(back, jnp.float32),
        ),
        in_specs=[WHOLE] * 4,
        out_specs=(pl.BlockSpec(memory_space=pl.ANY), WHOLE),
        scratch_shapes=[
            pltpu.VMEM((C * C, P_SIZE), jnp.float32),
            pltpu.VMEM((SIDE, SIDE, 2 * rows, P_SIZE), jnp.bfloat16),
            pltpu.VMEM((SIDE, SIDE, 2 * rows, P_SIZE), jnp.bfloat16),
            pltpu.SemaphoreType.DMA((2,)),
        ],
        compiler_params=pltpu.CompilerParams(vmem_limit_bytes=16 * 1024 * 1024),
        cost_estimate=pl.CostEstimate(flops=200_000_000, bytes_accessed=2_000_000, transcendentals=0),
    )(arrived.reshape(columns, WIDE), cotan_arrived, left_cols, grad_right)

    parts = lax.all_to_all(message.reshape(planes, 4 * rows, P_SIZE), ("y", "z"), 0, 0, tiled=True)

    terms, arrived = lax.optimization_barrier((terms, arrived))
    right_all = arrived.reshape(SIDE, SIDE, HALVES, ROW_DEV, WIDE).transpose(2, 1, 0, 3, 4).reshape(columns, WIDE)
    pair, back_hi, back_lo = pl.pallas_call(
        pair_kernel,
        out_shape=(
            jax.ShapeDtypeStruct((ROW_DEV, columns, P_SIZE), jnp.float32),
            jax.ShapeDtypeStruct(back, jnp.bfloat16),
            jax.ShapeDtypeStruct(back, jnp.bfloat16),
        ),
        in_specs=[WHOLE] * 4,
        out_specs=(WHOLE,) * 3,
        compiler_params=pltpu.CompilerParams(vmem_limit_bytes=16 * 1024 * 1024),
        cost_estimate=pl.CostEstimate(flops=150_000_000, bytes_accessed=2_000_000, transcendentals=0),
    )(right_all, mixed_hi, mixed_lo, terms)
    cols = columns // seq
    here = lax.axis_index("seq")

    def columns_of(owner):
        return lax.dynamic_slice_in_dim(pair, owner * cols, cols, 1)

    pair_sum = columns_of(here)
    for step in range(1, seq):
        sent = columns_of(lax.bitwise_xor(here, jnp.int32(step)))
        pair_sum = pair_sum + lax.ppermute(sent, "seq", [(q, q ^ step) for q in range(seq)])
    pair_update = (pair_sum * scale + out_bias).astype(jnp.bfloat16)
    back_hi, back_lo = (term.reshape(ROW_DEV, SEQ_DEV, C, P_SIZE) for term in (back_hi, back_lo))
    grad_left = dot32("isyk,xyk->isx", back_hi, weight) + dot32("isyk,xyk->isx", back_lo, weight)
    grad_left = (grad_left * scale).reshape(ROW_DEV, WIDE)

    parts, pair_update, grad_left = lax.optimization_barrier((parts, pair_update, grad_left))
    last = pl.pallas_call(
        middle_kernel,
        out_shape=jax.ShapeDtypeStruct((HALVES * seq, 2 * rows, P_SIZE), jnp.float32),
        in_specs=[pl.BlockSpec(memory_space=pltpu.SMEM), WHOLE],
        out_specs=WHOLE,
        compiler_params=pltpu.CompilerParams(vmem_limit_bytes=8 * 1024 * 1024),
    )(here.reshape(1), parts)
    last = lax.all_to_all(last, ("half", "seq"), 0, 0, tiled=True)
    grad_weight, grad_right, grad_bias = pl.pallas_call(
        lambda *refs: closing_kernel(scale, *refs),
        out_shape=(
            jax.ShapeDtypeStruct((rows, P_SIZE), jnp.float32),
            jax.ShapeDtypeStruct((ROW_DEV, WIDE), jnp.float32),
            jax.ShapeDtypeStruct((1, P_SIZE), jnp.float32),
        ),
        in_specs=[WHOLE],
        out_specs=(WHOLE,) * 3,
        compiler_params=pltpu.CompilerParams(vmem_limit_bytes=8 * 1024 * 1024),
    )(last)
    return pair_update, grad_left, grad_right, grad_weight, grad_bias[0]


def solution(mesh):
    res, seq = mesh.devices.shape
    fine = Mesh(mesh.devices.reshape(HALVES, SIDE, res // HALVES // SIDE, seq), ("half", "z", "y", "seq"))
    across = ("half", "z", "y")
    return jax.shard_map(
        on_device,
        mesh=fine,
        in_specs=(P(across, "seq"), P(across, "seq"), P(across, None, None), P(), P()),
        out_specs=(P(across, "seq", None), P(across, "seq"), P(across, "seq"), P(across, None), P()),
        check_vma=False,
    )
```

```python
import jax
import jax.numpy as jnp
from jax import lax
from jax.experimental import pallas as pl
from jax.experimental.pallas import tpu as pltpu
from jax.sharding import Mesh
from jax.sharding import PartitionSpec as P

C = 32
P_SIZE = 128
SEQ_DEV = 16
ROW_DEV = 2
WIDE = SEQ_DEV * C
HALVES = 2
SIDE = 8
WHOLE = pl.BlockSpec(memory_space=pltpu.VMEM)


def split_in_two(value):
    high = value.astype(jnp.bfloat16)
    return high, (value - high.astype(jnp.float32)).astype(jnp.bfloat16)


def dot32(form, a, b):
    return jnp.einsum(form, a, b, preferred_element_type=jnp.float32)


def opening_kernel(right, out, block, done):
    block[...] = jnp.broadcast_to(right[...][None], block.shape)
    size = block.shape[0]
    copies = [
        pltpu.make_async_copy(block, out.at[pl.ds(size * n, size)], done.at[n]) for n in range(out.shape[0] // size)
    ]
    for copy in copies:
        copy.start()
    for copy in copies:
        copy.wait()


def right_kernel(place, cotan, mixed_hi, mixed_lo, kept, sent):
    total = jnp.zeros((cotan.shape[1], WIDE), jnp.float32)
    for i in range(ROW_DEV):
        for mixed in (mixed_hi, mixed_lo):
            total += lax.dot_general(cotan[i], mixed[i], (((1,), (1,)), ((), ())), preferred_element_type=jnp.float32)
    low, high = total[:, : WIDE // 2], total[:, WIDE // 2 :]
    kept[...] = jnp.where(place[0] == 0, low, high)
    sent[...] = jnp.where(place[0] == 0, high, low).astype(jnp.bfloat16)


def packing_kernel(kept, got, out, total):
    blocks = kept.shape[1] // P_SIZE
    lines = ROW_DEV * blocks * HALVES
    planes = out.shape[0] // lines
    for m in range(blocks):
        cut = slice(m * P_SIZE, (m + 1) * P_SIZE)
        total[m] = kept[:, cut] + got[:, cut].astype(jnp.float32)
        for half in range(HALVES):
            for t in range(ROW_DEV):
                out[pl.ds((half * ROW_DEV + t) * blocks + m, planes, stride=lines), :] = total[
                    m, pl.ds(half * planes * ROW_DEV + t, planes, stride=ROW_DEV), :
                ]


def products_kernel(right, cotan, left_cols, grad_right, message, back, weight, own, other, done):
    both = jnp.concatenate([cotan[0], cotan[1]], axis=1)
    planes, lines = SIDE * SIDE, own.shape[2] // 2
    total = jnp.sum(both.astype(jnp.float32), axis=0, keepdims=True)
    total = total[:, :P_SIZE] + total[:, P_SIZE:]
    high = total.astype(jnp.bfloat16).astype(jnp.float32)
    line = lax.broadcasted_iota(jnp.int32, (lines, P_SIZE), 0)
    bias = jnp.where(line == 0, high, jnp.where(line == 1, total - high, 0.0))
    bias = jnp.broadcast_to(bias[None], (planes, lines, P_SIZE))
    tiles = jnp.concatenate([grad_right[...].reshape(planes, lines, P_SIZE), bias], axis=1).astype(jnp.bfloat16)
    for z in range(SIDE):
        other[z] = tiles[z * SIDE : (z + 1) * SIDE]
    first = pltpu.make_async_copy(other, message.at[:, :, pl.ds(2 * lines, 2 * lines)], done.at[0])
    first.start()

    terms = lax.dot_general(right[...], both, (((0,), (0,)), ((), ())), preferred_element_type=jnp.float32)
    back[0] = terms[:, :P_SIZE]
    back[1] = terms[:, P_SIZE:]
    lhs = left_cols[...]
    group = 8
    for y0 in range(0, C, group):
        columns = []
        for y in range(y0, y0 + group):
            parts = []
            for i in range(ROW_DEV):
                parts += split_in_two(back[i, pl.ds(y, SEQ_DEV, stride=C), :])
            columns.append(jnp.concatenate(parts, axis=0))
        terms = jnp.dot(lhs, jnp.concatenate(columns, axis=1), preferred_element_type=jnp.float32)
        for n in range(group):
            weight[pl.ds(y0 + n, C, stride=C), :] = terms[:, n * P_SIZE : (n + 1) * P_SIZE]
    halves = weight[...].reshape(HALVES, planes, lines, P_SIZE)
    tiles = jnp.concatenate([halves[0], halves[1]], axis=1).astype(jnp.bfloat16)
    for z in range(SIDE):
        own[z] = tiles[z * SIDE : (z + 1) * SIDE]
    second = pltpu.make_async_copy(own, message.at[:, :, pl.ds(0, 2 * lines)], done.at[1])
    second.start()
    first.wait()
    second.wait()


def pair_kernel(right, mixed_hi, mixed_lo, back, pair, back_hi, back_lo):
    rows = right[...]
    for i in range(ROW_DEV):
        pair[i] = jnp.dot(rows, mixed_hi[i], preferred_element_type=jnp.float32) + jnp.dot(
            rows, mixed_lo[i], preferred_element_type=jnp.float32
        )
        back_hi[i], back_lo[i] = split_in_two(back[i])


def middle_kernel(place, parts, out):
    total = jnp.sum(parts[...].astype(jnp.float32), axis=0)
    rows = total.shape[0] // 4
    seq = out.shape[0] // HALVES
    right, bias = total[2 * rows : 3 * rows], total[3 * rows : 3 * rows + rows // 2]
    rights = [right[: rows // 2], right[rows // 2 :]]
    for half in range(HALVES):
        mine = total[half * rows : (half + 1) * rows]
        for q in range(seq):
            out[half * seq + q, :rows] = mine
            mine_too = jnp.where(place[0] == q, rights[half], 0.0)
            out[half * seq + q, rows:] = jnp.concatenate([mine_too, bias], axis=0)


def closing_kernel(scale, parts, weight, right, bias):
    rows = weight.shape[0]
    seq = parts.shape[0] // HALVES
    sums = [jnp.sum(parts[half * seq : (half + 1) * seq], axis=0) * scale for half in range(HALVES)]
    weight[...] = sums[0][:rows] + sums[1][:rows]
    pieces = (sums[0] + sums[1])[rows + rows // 2 :]
    bias[...] = (pieces[0:1] + pieces[1:2]) * (1.0 / (scale * seq))
    blocks = WIDE // HALVES // P_SIZE
    for half in range(HALVES):
        for t in range(ROW_DEV):
            for m in range(blocks):
                at, to = rows + t * blocks + m, (half * blocks + m) * P_SIZE
                right[t : t + 1, to : to + P_SIZE] = sums[half][at : at + 1]


def on_device(left_proj, right_proj, pair_cotangent, out_weight, out_bias):
    planes = SIDE * SIDE
    seq = lax.axis_size("seq")
    res = HALVES * planes
    scale = 1.0 / (SEQ_DEV * seq)
    rows = C * C // res
    columns = res * ROW_DEV
    left_rows = left_proj.reshape(ROW_DEV, SEQ_DEV, C)
    weight = out_weight.reshape(C, C, P_SIZE)

    opening = pl.pallas_call(
        opening_kernel,
        out_shape=jax.ShapeDtypeStruct((res, ROW_DEV, WIDE), jnp.bfloat16),
        in_specs=[WHOLE],
        out_specs=pl.BlockSpec(memory_space=pl.ANY),
        scratch_shapes=[pltpu.VMEM((16, ROW_DEV, WIDE), jnp.bfloat16), pltpu.SemaphoreType.DMA((res // 16,))],
    )(right_proj)
    arrived = lax.all_to_all(opening, ("y", "z", "half"), 0, 0, tiled=True)
    cotan_arrived = pair_cotangent.reshape(ROW_DEV, HALVES, SIDE, SIDE, ROW_DEV, P_SIZE)
    cotan_arrived = cotan_arrived.transpose(0, 3, 2, 1, 4, 5).reshape(pair_cotangent.shape)

    mixed = dot32("isx,xyk->isyk", left_rows, weight)
    high = lax.reduce_precision(mixed, 8, 7)
    mixed_hi, mixed_lo = high.astype(jnp.bfloat16), (mixed - high).astype(jnp.bfloat16)
    back = (ROW_DEV, WIDE, P_SIZE)
    mixed_hi, mixed_lo = mixed_hi.reshape(back), mixed_lo.reshape(back)
    half_wide = jax.ShapeDtypeStruct((columns, WIDE // HALVES), jnp.float32)
    kept, sent = pl.pallas_call(
        right_kernel,
        out_shape=(half_wide, jax.ShapeDtypeStruct(half_wide.shape, jnp.bfloat16)),
        in_specs=[pl.BlockSpec(memory_space=pltpu.SMEM)] + [WHOLE] * 3,
        out_specs=(WHOLE,) * 2,
        compiler_params=pltpu.CompilerParams(vmem_limit_bytes=16 * 1024 * 1024),
        cost_estimate=pl.CostEstimate(flops=150_000_000, bytes_accessed=1_000_000, transcendentals=0),
    )(lax.axis_index("half").reshape(1), pair_cotangent, mixed_hi, mixed_lo)
    got = lax.ppermute(sent, "half", [(0, 1), (1, 0)])
    grad_right = pl.pallas_call(
        packing_kernel,
        out_shape=jax.ShapeDtypeStruct((columns * WIDE // HALVES // P_SIZE, P_SIZE), jnp.float32),
        in_specs=[WHOLE] * 2,
        out_specs=WHOLE,
        scratch_shapes=[pltpu.VMEM((WIDE // HALVES // P_SIZE, columns, P_SIZE), jnp.float32)],
        compiler_params=pltpu.CompilerParams(vmem_limit_bytes=16 * 1024 * 1024),
        cost_estimate=pl.CostEstimate(flops=100_000, bytes_accessed=1_000_000, transcendentals=0),
    )(kept, got)
    left_cols = jnp.broadcast_to(left_rows.transpose(2, 0, 1)[:, :, None], (C, ROW_DEV, 2, SEQ_DEV))
    left_cols = left_cols.reshape(C, ROW_DEV * 2 * SEQ_DEV)

    message, terms = pl.pallas_call(
        products_kernel,
        out_shape=(
            jax.ShapeDtypeStruct((SIDE, SIDE, 4 * rows, P_SIZE), jnp.bfloat16),
            jax.ShapeDtypeStruct(back, jnp.float32),
        ),
        in_specs=[WHOLE] * 4,
        out_specs=(pl.BlockSpec(memory_space=pl.ANY), WHOLE),
        scratch_shapes=[
            pltpu.VMEM((C * C, P_SIZE), jnp.float32),
            pltpu.VMEM((SIDE, SIDE, 2 * rows, P_SIZE), jnp.bfloat16),
            pltpu.VMEM((SIDE, SIDE, 2 * rows, P_SIZE), jnp.bfloat16),
            pltpu.SemaphoreType.DMA((2,)),
        ],
        compiler_params=pltpu.CompilerParams(vmem_limit_bytes=16 * 1024 * 1024),
        cost_estimate=pl.CostEstimate(flops=200_000_000, bytes_accessed=2_000_000, transcendentals=0),
    )(arrived.reshape(columns, WIDE), cotan_arrived, left_cols, grad_right)

    parts = lax.all_to_all(message.reshape(planes, 4 * rows, P_SIZE), ("z", "y"), 0, 0, tiled=True)

    terms, arrived = lax.optimization_barrier((terms, arrived))
    right_all = arrived.reshape(SIDE, SIDE, HALVES, ROW_DEV, WIDE).transpose(2, 1, 0, 3, 4).reshape(columns, WIDE)
    pair, back_hi, back_lo = pl.pallas_call(
        pair_kernel,
        out_shape=(
            jax.ShapeDtypeStruct((ROW_DEV, columns, P_SIZE), jnp.float32),
            jax.ShapeDtypeStruct(back, jnp.bfloat16),
            jax.ShapeDtypeStruct(back, jnp.bfloat16),
        ),
        in_specs=[WHOLE] * 4,
        out_specs=(WHOLE,) * 3,
        compiler_params=pltpu.CompilerParams(vmem_limit_bytes=16 * 1024 * 1024),
        cost_estimate=pl.CostEstimate(flops=150_000_000, bytes_accessed=2_000_000, transcendentals=0),
    )(right_all, mixed_hi, mixed_lo, terms)
    cols = columns // seq
    here = lax.axis_index("seq")

    def columns_of(owner):
        return lax.dynamic_slice_in_dim(pair, owner * cols, cols, 1)

    pair_sum = columns_of(here)
    for step in range(1, seq):
        sent = columns_of(lax.bitwise_xor(here, jnp.int32(step)))
        pair_sum = pair_sum + lax.ppermute(sent, "seq", [(q, q ^ step) for q in range(seq)])
    pair_update = (pair_sum * scale + out_bias).astype(jnp.bfloat16)
    back_hi, back_lo = (term.reshape(ROW_DEV, SEQ_DEV, C, P_SIZE) for term in (back_hi, back_lo))
    grad_left = dot32("isyk,xyk->isx", back_hi, weight) + dot32("isyk,xyk->isx", back_lo, weight)
    grad_left = (grad_left * scale).reshape(ROW_DEV, WIDE)

    parts, pair_update, grad_left = lax.optimization_barrier((parts, pair_update, grad_left))
    last = pl.pallas_call(
        middle_kernel,
        out_shape=jax.ShapeDtypeStruct((HALVES * seq, 2 * rows, P_SIZE), jnp.float32),
        in_specs=[pl.BlockSpec(memory_space=pltpu.SMEM), WHOLE],
        out_specs=WHOLE,
        compiler_params=pltpu.CompilerParams(vmem_limit_bytes=8 * 1024 * 1024),
    )(here.reshape(1), parts)
    last = lax.all_to_all(last, ("half", "seq"), 0, 0, tiled=True)
    grad_weight, grad_right, grad_bias = pl.pallas_call(
        lambda *refs: closing_kernel(scale, *refs),
        out_shape=(
            jax.ShapeDtypeStruct((rows, P_SIZE), jnp.float32),
            jax.ShapeDtypeStruct((ROW_DEV, WIDE), jnp.float32),
            jax.ShapeDtypeStruct((1, P_SIZE), jnp.float32),
        ),
        in_specs=[WHOLE],
        out_specs=(WHOLE,) * 3,
        compiler_params=pltpu.CompilerParams(vmem_limit_bytes=8 * 1024 * 1024),
    )(last)
    return pair_update, grad_left, grad_right, grad_weight, grad_bias[0]


def solution(mesh):
    res, seq = mesh.devices.shape
    fine = Mesh(mesh.devices.reshape(HALVES, SIDE, res // HALVES // SIDE, seq), ("half", "z", "y", "seq"))
    across = ("half", "z", "y")
    return jax.shard_map(
        on_device,
        mesh=fine,
        in_specs=(P(across, "seq"), P(across, "seq"), P(across, None, None), P(), P()),
        out_specs=(P(across, "seq", None), P(across, "seq"), P(across, "seq"), P(across, None), P()),
        check_vma=False,
    )
```

```python
import jax
import jax.numpy as jnp
from jax import lax
from jax.experimental import pallas as pl
from jax.experimental.pallas import tpu as pltpu
from jax.sharding import Mesh
from jax.sharding import PartitionSpec as P

C = 32
P_SIZE = 128
SEQ_DEV = 16
ROW_DEV = 2
WIDE = SEQ_DEV * C
HALVES = 2
SIDE = 8
WHOLE = pl.BlockSpec(memory_space=pltpu.VMEM)


def split_in_two(value):
    high = value.astype(jnp.bfloat16)
    return high, (value - high.astype(jnp.float32)).astype(jnp.bfloat16)


def dot32(form, a, b):
    return jnp.einsum(form, a, b, preferred_element_type=jnp.float32)


def opening_kernel(right, out, block, done):
    block[...] = jnp.broadcast_to(right[...][None], block.shape)
    size = block.shape[0]
    copies = [
        pltpu.make_async_copy(block, out.at[pl.ds(size * n, size)], done.at[n]) for n in range(out.shape[0] // size)
    ]
    for copy in copies:
        copy.start()
    for copy in copies:
        copy.wait()


def right_kernel(place, cotan, mixed_hi, mixed_lo, kept, sent):
    total = jnp.zeros((cotan.shape[1], WIDE), jnp.float32)
    for i in range(ROW_DEV):
        for mixed in (mixed_hi, mixed_lo):
            total += lax.dot_general(cotan[i], mixed[i], (((1,), (1,)), ((), ())), preferred_element_type=jnp.float32)
    low, high = total[:, : WIDE // 2], total[:, WIDE // 2 :]
    kept[...] = jnp.where(place[0] == 0, low, high)
    sent[...] = jnp.where(place[0] == 0, high, low).astype(jnp.bfloat16)


def packing_kernel(kept, got, out, total):
    blocks = kept.shape[1] // P_SIZE
    lines = ROW_DEV * blocks * HALVES
    planes = out.shape[0] // lines
    for m in range(blocks):
        cut = slice(m * P_SIZE, (m + 1) * P_SIZE)
        total[m] = kept[:, cut] + got[:, cut].astype(jnp.float32)
        for half in range(HALVES):
            for t in range(ROW_DEV):
                out[pl.ds((half * ROW_DEV + t) * blocks + m, planes, stride=lines), :] = total[
                    m, pl.ds(half * planes * ROW_DEV + t, planes, stride=ROW_DEV), :
                ]


def products_kernel(right, cotan, left_cols, grad_right, message, back, weight, own, other, done):
    both = jnp.concatenate([cotan[0], cotan[1]], axis=1)
    planes, lines = SIDE * SIDE, own.shape[2] // 2
    total = jnp.sum(both.astype(jnp.float32), axis=0, keepdims=True)
    total = total[:, :P_SIZE] + total[:, P_SIZE:]
    high = total.astype(jnp.bfloat16).astype(jnp.float32)
    line = lax.broadcasted_iota(jnp.int32, (lines, P_SIZE), 0)
    bias = jnp.where(line == 0, high, jnp.where(line == 1, total - high, 0.0))
    bias = jnp.broadcast_to(bias[None], (planes, lines, P_SIZE))
    tiles = jnp.concatenate([grad_right[...].reshape(planes, lines, P_SIZE), bias], axis=1).astype(jnp.bfloat16)
    for z in range(SIDE):
        other[z] = tiles[z * SIDE : (z + 1) * SIDE]
    first = pltpu.make_async_copy(other, message.at[:, :, pl.ds(2 * lines, 2 * lines)], done.at[0])
    first.start()

    terms = lax.dot_general(right[...], both, (((0,), (0,)), ((), ())), preferred_element_type=jnp.float32)
    back[0] = terms[:, :P_SIZE]
    back[1] = terms[:, P_SIZE:]
    lhs = left_cols[...]
    group = 8
    for y0 in range(0, C, group):
        columns = []
        for y in range(y0, y0 + group):
            parts = []
            for i in range(ROW_DEV):
                parts += split_in_two(back[i, pl.ds(y, SEQ_DEV, stride=C), :])
            columns.append(jnp.concatenate(parts, axis=0))
        terms = jnp.dot(lhs, jnp.concatenate(columns, axis=1), preferred_element_type=jnp.float32)
        for n in range(group):
            weight[pl.ds(y0 + n, C, stride=C), :] = terms[:, n * P_SIZE : (n + 1) * P_SIZE]
    halves = weight[...].reshape(HALVES, planes, lines, P_SIZE)
    tiles = jnp.concatenate([halves[0], halves[1]], axis=1).astype(jnp.bfloat16)
    for z in range(SIDE):
        own[z] = tiles[z * SIDE : (z + 1) * SIDE]
    second = pltpu.make_async_copy(own, message.at[:, :, pl.ds(0, 2 * lines)], done.at[1])
    second.start()
    first.wait()
    second.wait()


def pair_kernel(right, mixed_hi, mixed_lo, back, pair, back_hi, back_lo):
    rows = right[...]
    for i in range(ROW_DEV):
        pair[i] = jnp.dot(rows, mixed_hi[i], preferred_element_type=jnp.float32) + jnp.dot(
            rows, mixed_lo[i], preferred_element_type=jnp.float32
        )
        back_hi[i], back_lo[i] = split_in_two(back[i])


def middle_kernel(place, parts, out):
    total = jnp.sum(parts[...].astype(jnp.float32), axis=0)
    rows = total.shape[0] // 4
    seq = out.shape[0] // HALVES
    right, bias = total[2 * rows : 3 * rows], total[3 * rows : 3 * rows + rows // 2]
    rights = [right[: rows // 2], right[rows // 2 :]]
    for half in range(HALVES):
        mine = total[half * rows : (half + 1) * rows]
        for q in range(seq):
            out[q * HALVES + half, :rows] = mine
            mine_too = jnp.where(place[0] == q, rights[half], 0.0)
            out[q * HALVES + half, rows:] = jnp.concatenate([mine_too, bias], axis=0)


def closing_kernel(scale, parts, weight, right, bias):
    rows = weight.shape[0]
    seq = parts.shape[0] // HALVES
    sums = [sum(parts[q * HALVES + half] for q in range(seq)) * scale for half in range(HALVES)]
    weight[...] = sums[0][:rows] + sums[1][:rows]
    pieces = (sums[0] + sums[1])[rows + rows // 2 :]
    bias[...] = (pieces[0:1] + pieces[1:2]) * (1.0 / (scale * seq))
    blocks = WIDE // HALVES // P_SIZE
    for half in range(HALVES):
        for t in range(ROW_DEV):
            for m in range(blocks):
                at, to = rows + t * blocks + m, (half * blocks + m) * P_SIZE
                right[t : t + 1, to : to + P_SIZE] = sums[half][at : at + 1]


def on_device(left_proj, right_proj, pair_cotangent, out_weight, out_bias):
    planes = SIDE * SIDE
    seq = lax.axis_size("seq")
    res = HALVES * planes
    scale = 1.0 / (SEQ_DEV * seq)
    rows = C * C // res
    columns = res * ROW_DEV
    left_rows = left_proj.reshape(ROW_DEV, SEQ_DEV, C)
    weight = out_weight.reshape(C, C, P_SIZE)

    opening = pl.pallas_call(
        opening_kernel,
        out_shape=jax.ShapeDtypeStruct((res, ROW_DEV, WIDE), jnp.bfloat16),
        in_specs=[WHOLE],
        out_specs=pl.BlockSpec(memory_space=pl.ANY),
        scratch_shapes=[pltpu.VMEM((16, ROW_DEV, WIDE), jnp.bfloat16), pltpu.SemaphoreType.DMA((res // 16,))],
    )(right_proj)
    arrived = lax.all_to_all(opening, ("y", "z", "half"), 0, 0, tiled=True)
    cotan_arrived = pair_cotangent.reshape(ROW_DEV, HALVES, SIDE, SIDE, ROW_DEV, P_SIZE)
    cotan_arrived = cotan_arrived.transpose(0, 3, 2, 1, 4, 5).reshape(pair_cotangent.shape)

    mixed = dot32("isx,xyk->isyk", left_rows, weight)
    high = lax.reduce_precision(mixed, 8, 7)
    mixed_hi, mixed_lo = high.astype(jnp.bfloat16), (mixed - high).astype(jnp.bfloat16)
    back = (ROW_DEV, WIDE, P_SIZE)
    mixed_hi, mixed_lo = mixed_hi.reshape(back), mixed_lo.reshape(back)
    half_wide = jax.ShapeDtypeStruct((columns, WIDE // HALVES), jnp.float32)
    kept, sent = pl.pallas_call(
        right_kernel,
        out_shape=(half_wide, jax.ShapeDtypeStruct(half_wide.shape, jnp.bfloat16)),
        in_specs=[pl.BlockSpec(memory_space=pltpu.SMEM)] + [WHOLE] * 3,
        out_specs=(WHOLE,) * 2,
        compiler_params=pltpu.CompilerParams(vmem_limit_bytes=16 * 1024 * 1024),
        cost_estimate=pl.CostEstimate(flops=150_000_000, bytes_accessed=1_000_000, transcendentals=0),
    )(lax.axis_index("half").reshape(1), pair_cotangent, mixed_hi, mixed_lo)
    got = lax.ppermute(sent, "half", [(0, 1), (1, 0)])
    grad_right = pl.pallas_call(
        packing_kernel,
        out_shape=jax.ShapeDtypeStruct((columns * WIDE // HALVES // P_SIZE, P_SIZE), jnp.float32),
        in_specs=[WHOLE] * 2,
        out_specs=WHOLE,
        scratch_shapes=[pltpu.VMEM((WIDE // HALVES // P_SIZE, columns, P_SIZE), jnp.float32)],
        compiler_params=pltpu.CompilerParams(vmem_limit_bytes=16 * 1024 * 1024),
        cost_estimate=pl.CostEstimate(flops=100_000, bytes_accessed=1_000_000, transcendentals=0),
    )(kept, got)
    left_cols = jnp.broadcast_to(left_rows.transpose(2, 0, 1)[:, :, None], (C, ROW_DEV, 2, SEQ_DEV))
    left_cols = left_cols.reshape(C, ROW_DEV * 2 * SEQ_DEV)

    message, terms = pl.pallas_call(
        products_kernel,
        out_shape=(
            jax.ShapeDtypeStruct((SIDE, SIDE, 4 * rows, P_SIZE), jnp.bfloat16),
            jax.ShapeDtypeStruct(back, jnp.float32),
        ),
        in_specs=[WHOLE] * 4,
        out_specs=(pl.BlockSpec(memory_space=pl.ANY), WHOLE),
        scratch_shapes=[
            pltpu.VMEM((C * C, P_SIZE), jnp.float32),
            pltpu.VMEM((SIDE, SIDE, 2 * rows, P_SIZE), jnp.bfloat16),
            pltpu.VMEM((SIDE, SIDE, 2 * rows, P_SIZE), jnp.bfloat16),
            pltpu.SemaphoreType.DMA((2,)),
        ],
        compiler_params=pltpu.CompilerParams(vmem_limit_bytes=16 * 1024 * 1024),
        cost_estimate=pl.CostEstimate(flops=200_000_000, bytes_accessed=2_000_000, transcendentals=0),
    )(arrived.reshape(columns, WIDE), cotan_arrived, left_cols, grad_right)

    parts = lax.all_to_all(message.reshape(planes, 4 * rows, P_SIZE), ("z", "y"), 0, 0, tiled=True)

    terms, arrived = lax.optimization_barrier((terms, arrived))
    right_all = arrived.reshape(SIDE, SIDE, HALVES, ROW_DEV, WIDE).transpose(2, 1, 0, 3, 4).reshape(columns, WIDE)
    pair, back_hi, back_lo = pl.pallas_call(
        pair_kernel,
        out_shape=(
            jax.ShapeDtypeStruct((ROW_DEV, columns, P_SIZE), jnp.float32),
            jax.ShapeDtypeStruct(back, jnp.bfloat16),
            jax.ShapeDtypeStruct(back, jnp.bfloat16),
        ),
        in_specs=[WHOLE] * 4,
        out_specs=(WHOLE,) * 3,
        compiler_params=pltpu.CompilerParams(vmem_limit_bytes=16 * 1024 * 1024),
        cost_estimate=pl.CostEstimate(flops=150_000_000, bytes_accessed=2_000_000, transcendentals=0),
    )(right_all, mixed_hi, mixed_lo, terms)
    cols = columns // seq
    here = lax.axis_index("seq")

    def columns_of(owner):
        return lax.dynamic_slice_in_dim(pair, owner * cols, cols, 1)

    pair_sum = columns_of(here)
    for step in range(1, seq):
        sent = columns_of(lax.bitwise_xor(here, jnp.int32(step)))
        pair_sum = pair_sum + lax.ppermute(sent, "seq", [(q, q ^ step) for q in range(seq)])
    pair_update = (pair_sum * scale + out_bias).astype(jnp.bfloat16)
    back_hi, back_lo = (term.reshape(ROW_DEV, SEQ_DEV, C, P_SIZE) for term in (back_hi, back_lo))
    grad_left = dot32("isyk,xyk->isx", back_hi, weight) + dot32("isyk,xyk->isx", back_lo, weight)
    grad_left = (grad_left * scale).reshape(ROW_DEV, WIDE)

    parts, pair_update, grad_left = lax.optimization_barrier((parts, pair_update, grad_left))
    last = pl.pallas_call(
        middle_kernel,
        out_shape=jax.ShapeDtypeStruct((HALVES * seq, 2 * rows, P_SIZE), jnp.float32),
        in_specs=[pl.BlockSpec(memory_space=pltpu.SMEM), WHOLE],
        out_specs=WHOLE,
        compiler_params=pltpu.CompilerParams(vmem_limit_bytes=8 * 1024 * 1024),
    )(here.reshape(1), parts)
    last = lax.all_to_all(last, ("seq", "half"), 0, 0, tiled=True)
    grad_weight, grad_right, grad_bias = pl.pallas_call(
        lambda *refs: closing_kernel(scale, *refs),
        out_shape=(
            jax.ShapeDtypeStruct((rows, P_SIZE), jnp.float32),
            jax.ShapeDtypeStruct((ROW_DEV, WIDE), jnp.float32),
            jax.ShapeDtypeStruct((1, P_SIZE), jnp.float32),
        ),
        in_specs=[WHOLE],
        out_specs=(WHOLE,) * 3,
        compiler_params=pltpu.CompilerParams(vmem_limit_bytes=8 * 1024 * 1024),
    )(last)
    return pair_update, grad_left, grad_right, grad_weight, grad_bias[0]


def solution(mesh):
    res, seq = mesh.devices.shape
    fine = Mesh(mesh.devices.reshape(HALVES, SIDE, res // HALVES // SIDE, seq), ("half", "z", "y", "seq"))
    across = ("half", "z", "y")
    return jax.shard_map(
        on_device,
        mesh=fine,
        in_specs=(P(across, "seq"), P(across, "seq"), P(across, None, None), P(), P()),
        out_specs=(P(across, "seq", None), P(across, "seq"), P(across, "seq"), P(across, None), P()),
        check_vma=False,
    )
```

```python
import jax
import jax.numpy as jnp
from jax import lax
from jax.experimental import pallas as pl
from jax.experimental.pallas import tpu as pltpu
from jax.sharding import Mesh
from jax.sharding import PartitionSpec as P

C = 32
P_SIZE = 128
SEQ_DEV = 16
ROW_DEV = 2
WIDE = SEQ_DEV * C
HALVES = 2
SIDE = 8
WHOLE = pl.BlockSpec(memory_space=pltpu.VMEM)


def split_in_two(value):
    high = value.astype(jnp.bfloat16)
    return high, (value - high.astype(jnp.float32)).astype(jnp.bfloat16)


def dot32(form, a, b):
    return jnp.einsum(form, a, b, preferred_element_type=jnp.float32)


def opening_kernel(right, out, block, done):
    block[...] = jnp.broadcast_to(right[...][None], block.shape)
    size = block.shape[0]
    copies = [
        pltpu.make_async_copy(block, out.at[pl.ds(size * n, size)], done.at[n]) for n in range(out.shape[0] // size)
    ]
    for copy in copies:
        copy.start()
    for copy in copies:
        copy.wait()


def right_kernel(place, cotan, mixed_hi, mixed_lo, kept, sent):
    total = jnp.zeros((cotan.shape[1], WIDE), jnp.float32)
    for i in range(ROW_DEV):
        for mixed in (mixed_hi, mixed_lo):
            total += lax.dot_general(cotan[i], mixed[i], (((1,), (1,)), ((), ())), preferred_element_type=jnp.float32)
    low, high = total[:, : WIDE // 2], total[:, WIDE // 2 :]
    kept[...] = jnp.where(place[0] == 0, low, high)
    sent[...] = jnp.where(place[0] == 0, high, low).astype(jnp.bfloat16)


def packing_kernel(kept, got, out, total):
    blocks = kept.shape[1] // P_SIZE
    lines = ROW_DEV * blocks * HALVES
    planes = out.shape[0] // lines
    for m in range(blocks):
        cut = slice(m * P_SIZE, (m + 1) * P_SIZE)
        total[m] = kept[:, cut] + got[:, cut].astype(jnp.float32)
        for half in range(HALVES):
            for t in range(ROW_DEV):
                out[pl.ds((half * ROW_DEV + t) * blocks + m, planes, stride=lines), :] = total[
                    m, pl.ds(half * planes * ROW_DEV + t, planes, stride=ROW_DEV), :
                ]


def products_kernel(right, cotan, left_cols, grad_right, message, back, weight, own, other, done):
    both = jnp.concatenate([cotan[0], cotan[1]], axis=1)
    planes, lines = SIDE * SIDE, own.shape[2] // 2
    total = jnp.sum(both.astype(jnp.float32), axis=0, keepdims=True)
    total = total[:, :P_SIZE] + total[:, P_SIZE:]
    high = total.astype(jnp.bfloat16).astype(jnp.float32)
    line = lax.broadcasted_iota(jnp.int32, (lines, P_SIZE), 0)
    bias = jnp.where(line == 0, high, jnp.where(line == 1, total - high, 0.0))
    bias = jnp.broadcast_to(bias[None], (planes, lines, P_SIZE))
    tiles = jnp.concatenate([grad_right[...].reshape(planes, lines, P_SIZE), bias], axis=1).astype(jnp.bfloat16)
    for z in range(SIDE):
        other[z] = tiles[z * SIDE : (z + 1) * SIDE]
    first = pltpu.make_async_copy(other, message.at[:, :, pl.ds(2 * lines, 2 * lines)], done.at[0])
    first.start()

    terms = lax.dot_general(right[...], both, (((0,), (0,)), ((), ())), preferred_element_type=jnp.float32)
    back[0] = terms[:, :P_SIZE]
    back[1] = terms[:, P_SIZE:]
    lhs = left_cols[...]
    group = 8
    for y0 in range(0, C, group):
        columns = []
        for y in range(y0, y0 + group):
            parts = []
            for i in range(ROW_DEV):
                parts += split_in_two(back[i, pl.ds(y, SEQ_DEV, stride=C), :])
            columns.append(jnp.concatenate(parts, axis=0))
        terms = jnp.dot(lhs, jnp.concatenate(columns, axis=1), preferred_element_type=jnp.float32)
        for n in range(group):
            weight[pl.ds(y0 + n, C, stride=C), :] = terms[:, n * P_SIZE : (n + 1) * P_SIZE]
    halves = weight[...].reshape(HALVES, planes, lines, P_SIZE)
    tiles = jnp.concatenate([halves[0], halves[1]], axis=1).astype(jnp.bfloat16)
    for z in range(SIDE):
        own[z] = tiles[z * SIDE : (z + 1) * SIDE]
    second = pltpu.make_async_copy(own, message.at[:, :, pl.ds(0, 2 * lines)], done.at[1])
    second.start()
    first.wait()
    second.wait()


def pair_kernel(right, mixed_hi, mixed_lo, back, pair, back_hi, back_lo):
    rows = right[...]
    for i in range(ROW_DEV):
        pair[i] = jnp.dot(rows, mixed_hi[i], preferred_element_type=jnp.float32) + jnp.dot(
            rows, mixed_lo[i], preferred_element_type=jnp.float32
        )
        back_hi[i], back_lo[i] = split_in_two(back[i])


def middle_kernel(place, parts, out):
    total = jnp.sum(parts[...].astype(jnp.float32), axis=0)
    rows = total.shape[0] // 4
    seq = out.shape[0] // HALVES
    right, bias = total[2 * rows : 3 * rows], total[3 * rows : 3 * rows + rows // 2]
    rights = [right[: rows // 2], right[rows // 2 :]]
    for half in range(HALVES):
        mine = total[half * rows : (half + 1) * rows]
        for q in range(seq):
            out[half * seq + q, :rows] = mine
            mine_too = jnp.where(place[0] == q, rights[half], 0.0)
            out[half * seq + q, rows:] = jnp.concatenate([mine_too, bias], axis=0)


def closing_kernel(scale, parts, weight, right, bias):
    rows = weight.shape[0]
    seq = parts.shape[0] // HALVES
    sums = [jnp.sum(parts[half * seq : (half + 1) * seq], axis=0) * scale for half in range(HALVES)]
    weight[...] = sums[0][:rows] + sums[1][:rows]
    pieces = (sums[0] + sums[1])[rows + rows // 2 :]
    bias[...] = (pieces[0:1] + pieces[1:2]) * (1.0 / (scale * seq))
    blocks = WIDE // HALVES // P_SIZE
    for half in range(HALVES):
        for t in range(ROW_DEV):
            for m in range(blocks):
                at, to = rows + t * blocks + m, (half * blocks + m) * P_SIZE
                right[t : t + 1, to : to + P_SIZE] = sums[half][at : at + 1]


def on_device(left_proj, right_proj, pair_cotangent, out_weight, out_bias):
    planes = SIDE * SIDE
    seq = lax.axis_size("seq")
    res = HALVES * planes
    scale = 1.0 / (SEQ_DEV * seq)
    rows = C * C // res
    columns = res * ROW_DEV
    left_rows = left_proj.reshape(ROW_DEV, SEQ_DEV, C)
    weight = out_weight.reshape(C, C, P_SIZE)

    opening = pl.pallas_call(
        opening_kernel,
        out_shape=jax.ShapeDtypeStruct((res, ROW_DEV, WIDE), jnp.bfloat16),
        in_specs=[WHOLE],
        out_specs=pl.BlockSpec(memory_space=pl.ANY),
        scratch_shapes=[pltpu.VMEM((32, ROW_DEV, WIDE), jnp.bfloat16), pltpu.SemaphoreType.DMA((res // 32,))],
    )(right_proj)
    arrived = lax.all_to_all(opening, ("y", "z", "half"), 0, 0, tiled=True)
    cotan_arrived = pair_cotangent.reshape(ROW_DEV, HALVES, SIDE, SIDE, ROW_DEV, P_SIZE)
    cotan_arrived = cotan_arrived.transpose(0, 3, 2, 1, 4, 5).reshape(pair_cotangent.shape)

    mixed = dot32("isx,xyk->isyk", left_rows, weight)
    high = lax.reduce_precision(mixed, 8, 7)
    mixed_hi, mixed_lo = high.astype(jnp.bfloat16), (mixed - high).astype(jnp.bfloat16)
    back = (ROW_DEV, WIDE, P_SIZE)
    mixed_hi, mixed_lo = mixed_hi.reshape(back), mixed_lo.reshape(back)
    half_wide = jax.ShapeDtypeStruct((columns, WIDE // HALVES), jnp.float32)
    kept, sent = pl.pallas_call(
        right_kernel,
        out_shape=(half_wide, jax.ShapeDtypeStruct(half_wide.shape, jnp.bfloat16)),
        in_specs=[pl.BlockSpec(memory_space=pltpu.SMEM)] + [WHOLE] * 3,
        out_specs=(WHOLE,) * 2,
        compiler_params=pltpu.CompilerParams(vmem_limit_bytes=16 * 1024 * 1024),
        cost_estimate=pl.CostEstimate(flops=150_000_000, bytes_accessed=1_000_000, transcendentals=0),
    )(lax.axis_index("half").reshape(1), pair_cotangent, mixed_hi, mixed_lo)
    got = lax.ppermute(sent, "half", [(0, 1), (1, 0)])
    grad_right = pl.pallas_call(
        packing_kernel,
        out_shape=jax.ShapeDtypeStruct((columns * WIDE // HALVES // P_SIZE, P_SIZE), jnp.float32),
        in_specs=[WHOLE] * 2,
        out_specs=WHOLE,
        scratch_shapes=[pltpu.VMEM((WIDE // HALVES // P_SIZE, columns, P_SIZE), jnp.float32)],
        compiler_params=pltpu.CompilerParams(vmem_limit_bytes=16 * 1024 * 1024),
        cost_estimate=pl.CostEstimate(flops=100_000, bytes_accessed=1_000_000, transcendentals=0),
    )(kept, got)
    left_cols = jnp.broadcast_to(left_rows.transpose(2, 0, 1)[:, :, None], (C, ROW_DEV, 2, SEQ_DEV))
    left_cols = left_cols.reshape(C, ROW_DEV * 2 * SEQ_DEV)

    message, terms = pl.pallas_call(
        products_kernel,
        out_shape=(
            jax.ShapeDtypeStruct((SIDE, SIDE, 4 * rows, P_SIZE), jnp.bfloat16),
            jax.ShapeDtypeStruct(back, jnp.float32),
        ),
        in_specs=[WHOLE] * 4,
        out_specs=(pl.BlockSpec(memory_space=pl.ANY), WHOLE),
        scratch_shapes=[
            pltpu.VMEM((C * C, P_SIZE), jnp.float32),
            pltpu.VMEM((SIDE, SIDE, 2 * rows, P_SIZE), jnp.bfloat16),
            pltpu.VMEM((SIDE, SIDE, 2 * rows, P_SIZE), jnp.bfloat16),
            pltpu.SemaphoreType.DMA((2,)),
        ],
        compiler_params=pltpu.CompilerParams(vmem_limit_bytes=16 * 1024 * 1024),
        cost_estimate=pl.CostEstimate(flops=200_000_000, bytes_accessed=2_000_000, transcendentals=0),
    )(arrived.reshape(columns, WIDE), cotan_arrived, left_cols, grad_right)

    parts = lax.all_to_all(message.reshape(planes, 4 * rows, P_SIZE), ("z", "y"), 0, 0, tiled=True)

    terms, arrived = lax.optimization_barrier((terms, arrived))
    right_all = arrived.reshape(SIDE, SIDE, HALVES, ROW_DEV, WIDE).transpose(2, 1, 0, 3, 4).reshape(columns, WIDE)
    pair, back_hi, back_lo = pl.pallas_call(
        pair_kernel,
        out_shape=(
            jax.ShapeDtypeStruct((ROW_DEV, columns, P_SIZE), jnp.float32),
            jax.ShapeDtypeStruct(back, jnp.bfloat16),
            jax.ShapeDtypeStruct(back, jnp.bfloat16),
        ),
        in_specs=[WHOLE] * 4,
        out_specs=(WHOLE,) * 3,
        compiler_params=pltpu.CompilerParams(vmem_limit_bytes=16 * 1024 * 1024),
        cost_estimate=pl.CostEstimate(flops=150_000_000, bytes_accessed=2_000_000, transcendentals=0),
    )(right_all, mixed_hi, mixed_lo, terms)
    cols = columns // seq
    here = lax.axis_index("seq")

    def columns_of(owner):
        return lax.dynamic_slice_in_dim(pair, owner * cols, cols, 1)

    pair_sum = columns_of(here)
    for step in range(1, seq):
        sent = columns_of(lax.bitwise_xor(here, jnp.int32(step)))
        pair_sum = pair_sum + lax.ppermute(sent, "seq", [(q, q ^ step) for q in range(seq)])
    pair_update = (pair_sum * scale + out_bias).astype(jnp.bfloat16)
    back_hi, back_lo = (term.reshape(ROW_DEV, SEQ_DEV, C, P_SIZE) for term in (back_hi, back_lo))
    grad_left = dot32("isyk,xyk->isx", back_hi, weight) + dot32("isyk,xyk->isx", back_lo, weight)
    grad_left = (grad_left * scale).reshape(ROW_DEV, WIDE)

    parts, pair_update, grad_left = lax.optimization_barrier((parts, pair_update, grad_left))
    last = pl.pallas_call(
        middle_kernel,
        out_shape=jax.ShapeDtypeStruct((HALVES * seq, 2 * rows, P_SIZE), jnp.float32),
        in_specs=[pl.BlockSpec(memory_space=pltpu.SMEM), WHOLE],
        out_specs=WHOLE,
        compiler_params=pltpu.CompilerParams(vmem_limit_bytes=8 * 1024 * 1024),
    )(here.reshape(1), parts)
    last = lax.all_to_all(last, ("half", "seq"), 0, 0, tiled=True)
    grad_weight, grad_right, grad_bias = pl.pallas_call(
        lambda *refs: closing_kernel(scale, *refs),
        out_shape=(
            jax.ShapeDtypeStruct((rows, P_SIZE), jnp.float32),
            jax.ShapeDtypeStruct((ROW_DEV, WIDE), jnp.float32),
            jax.ShapeDtypeStruct((1, P_SIZE), jnp.float32),
        ),
        in_specs=[WHOLE],
        out_specs=(WHOLE,) * 3,
        compiler_params=pltpu.CompilerParams(vmem_limit_bytes=8 * 1024 * 1024),
    )(last)
    return pair_update, grad_left, grad_right, grad_weight, grad_bias[0]


def solution(mesh):
    res, seq = mesh.devices.shape
    fine = Mesh(mesh.devices.reshape(HALVES, SIDE, res // HALVES // SIDE, seq), ("half", "z", "y", "seq"))
    across = ("half", "z", "y")
    return jax.shard_map(
        on_device,
        mesh=fine,
        in_specs=(P(across, "seq"), P(across, "seq"), P(across, None, None), P(), P()),
        out_specs=(P(across, "seq", None), P(across, "seq"), P(across, "seq"), P(across, None), P()),
        check_vma=False,
    )
```
